128 devices in a mesh: dp: 16 (over y_lo, z, core), seq: 8 (over x, y_hi).
Axes of the slice: x: 4, y: 4 (y_hi: 2, y_lo: 2; y = y_hi * 2 + y_lo), z: 4, core: 2. Of those that a mesh axis runs over, the one named last changes fastest.
Arguments:
- query: bfloat16 [16, 3072, 1536], P('dp', 'seq'), may hold values from -8 to 8
- key_states: bfloat16 [16, 3072, 1536], P('dp', 'seq'), may hold values from -8 to 8
- value_states: bfloat16 [16, 3072, 1536], P('dp', 'seq'), may hold values from -6 to 6
- grad_out: bfloat16 [16, 3072, 3072], P('dp', 'seq'), may hold values from -6 to 6
- w_out: bfloat16 [1536, 3072], P('dp'), may hold values from -0.15625 to 0.15625
- block_index: int32 [24, 24, 8], replicated, may hold values from 0 to 23, as said below
- block_count: int32 [24, 24], replicated, may hold values from 1 to 8, as said below
Outputs:
- grad_query: bfloat16 [16, 3072, 1536], P('dp', 'seq')
- grad_key: bfloat16 [16, 3072, 1536], P('dp', 'seq')
- grad_value: bfloat16 [16, 3072, 1536], P('dp', 'seq')
- grad_weight: float32 [1536, 3072], P(('seq', 'dp'))
The draws below stay inside these ranges and needn't reach their ends.
Inputs may be any that keep to these rules, and one draw needn't show every extreme that they name: `block_index`: entry 0 of row [h, i] is i; the 8 entries of a row are distinct blocks within circular distance 8 // 2 of i. `block_count`: every head has a query block with count 8.
All inputs are finite; a program needn't handle non-finite values.
Results may differ from the reference program's by a relative error of at most 0.022.
Values may be sent and summed in bfloat16 or wider, within the bound.
A program may use at most 128 MiB of HBM per device.

```python
import jax
import jax.numpy as jnp
from jax import lax

D = 3072
HEADS = 24
MAXB = 8
SEQ = 3072
BATCH = 16
TOKENS = 49152
HD = 1536
NB = 24


def offsets_table(width):
    steps = jnp.arange(width)
    return (steps + 1) // 2 * jnp.where(steps % 2 == 1, 1, -1)


def draw_block_index(key, part):
    keys = jax.random.split(jax.random.fold_in(key, 11), HEADS * NB)
    perms = jax.vmap(lambda single: jax.random.permutation(single, MAXB - 1))(keys)
    order = jnp.concatenate([jnp.zeros((HEADS * NB, 1), jnp.int32), perms.astype(jnp.int32) + 1], axis=1)
    offsets = offsets_table(MAXB)[order]
    blocks = jnp.tile(jnp.arange(NB), HEADS)[:, None]
    return ((blocks + offsets) % NB).reshape(HEADS, NB, MAXB).astype(jnp.int32)


def draw_block_count(key, part):
    first, second, third = jax.random.split(jax.random.fold_in(key, 13), 3)
    level = jax.random.randint(first, (HEADS, 1), MAXB // 2, MAXB + 1)
    lowest = jnp.maximum(level // 2, 1)
    spread = jax.random.randint(second, (HEADS, NB), 0, 1 << 20) % (level - lowest + 1)
    counts = lowest + spread
    fullest = jax.random.randint(third, (HEADS,), 0, NB)
    counts = jnp.where(jnp.arange(NB)[None, :] == fullest[:, None], MAXB, counts)
    return counts.astype(jnp.int32)


def base_noise(key):
    return jnp.clip(jax.random.normal(key, (BATCH, SEQ, HD), jnp.float32), -4.0, 4.0)


def draw_query(key, part):
    noise = base_noise(jax.random.fold_in(key, 1))
    return noise.astype(jnp.bfloat16)


def draw_key_states(key, part):
    noise = base_noise(jax.random.fold_in(key, 2))
    return noise.astype(jnp.bfloat16)


def shard_levels(stream_key, extent, pieces, least, largest):
    def one(axis_at, parts):
        steps = jax.random.uniform(jax.random.fold_in(jax.random.fold_in(stream_key, 6), axis_at), (parts,), jnp.float32, least / len(pieces), largest / len(pieces))
        return jnp.repeat(jnp.exp(steps), extent[axis_at] // parts).reshape((-1,) + (1,) * (len(extent) - axis_at - 1))

    loudness = one(*pieces[0])
    for cut in pieces[1:]:
        loudness = loudness * one(*cut)
    return loudness


def scatter_about(stream_key, dims, scale, bound, shards=(), held_as=jnp.bfloat16):
    loudness = shard_levels(stream_key, dims, shards, -0.22, 0.18) if shards else 1.0
    entries = jax.random.normal(stream_key, dims, jnp.float32) * scale * loudness
    return jnp.minimum(jnp.maximum(entries, -bound), bound).astype(held_as)


def setup_inputs(seed: int = 0) -> dict:
    key_of = jax.random.split(jax.random.key(seed), 8)
    return {
        "query": draw_query(jax.random.fold_in(key_of[7], 71), 0),
        "key_states": draw_key_states(jax.random.fold_in(key_of[7], 71), 0),
        "value_states": scatter_about(key_of[2], (BATCH, SEQ, HD), 1.0, 6.0, ((0, 16), (1, 8))),
        "grad_out": scatter_about(key_of[3], (BATCH, SEQ, D), 1.0, 6.0, ((0, 16), (1, 8))),
        "w_out": scatter_about(key_of[4], (HD, D), HD ** -0.5, 0.15625, ((0, 16),)),
        "block_index": draw_block_index(jax.random.fold_in(key_of[7], 71), 0),
        "block_count": draw_block_count(jax.random.fold_in(key_of[7], 71), 0),
    }


def block_attention(query_f, key_f, value_f, index, count):

    def one_head(q_head, k_head, v_head, ids_head, cnt_head):
        blocks = ids_head.shape[0]
        slots = ids_head.shape[1]
        width = q_head.shape[0] // blocks
        hdim = q_head.shape[1]
        scale_factor = hdim ** (-0.5)
        key_blocks = k_head.reshape(blocks, width, hdim)
        value_blocks = v_head.reshape(blocks, width, hdim)
        query_blocks = q_head.reshape(blocks, width, hdim)

        @jax.checkpoint
        def one_block(items):
            q_rows, ids, cnt = items
            keys = key_blocks[ids].reshape(slots * width, hdim).astype(jnp.bfloat16)
            values = value_blocks[ids].reshape(slots * width, hdim).astype(jnp.bfloat16)
            scores = lax.dot_general(q_rows.astype(jnp.bfloat16), keys, (((1,), (1,)), ((), ())), preferred_element_type=jnp.float32) * scale_factor
            live = jnp.broadcast_to((jnp.arange(slots) < cnt)[:, None], (slots, width)).reshape(-1)
            scores = jnp.where(live[None, :], scores, jnp.float32(-1e+30))
            top = lax.optimization_barrier(jnp.max(scores, axis=1, keepdims=True))
            weights = jnp.exp(scores - top)
            probs = weights / lax.optimization_barrier(jnp.sum(weights, axis=1, keepdims=True))
            return jnp.dot(probs.astype(jnp.bfloat16), values, preferred_element_type=jnp.float32)
        result = lax.map(one_block, (query_blocks, ids_head, cnt_head))
        return result.reshape(blocks * width, hdim)
    return jax.vmap(one_head, in_axes=(1, 1, 1, 0, 0), out_axes=1)(query_f, key_f, value_f, index, count)

def video_backward(query_v, key_v, value_v, d_attn, index, count):
    seqlen, hd_all = query_v.shape
    heads = index.shape[0]
    hdim = hd_all // heads

    def shape_heads(array):
        return array.astype(jnp.float32).reshape(seqlen, heads, hdim)

    def attend(q_arr, k_arr, v_arr):
        return block_attention(q_arr, k_arr, v_arr, index, count)

    def flatten(array):
        return array.reshape(seqlen, hd_all).astype(jnp.bfloat16)
    attn, pull = jax.vjp(attend, shape_heads(query_v), shape_heads(key_v), shape_heads(value_v))
    grad_q, grad_k, grad_v = pull(shape_heads(d_attn))
    return (flatten(attn), flatten(grad_q), flatten(grad_k), flatten(grad_v))

def reference(query, key_states, value_states, grad_out, w_out, block_index, block_count):

    def one_video(total, items):
        q_vid, k_vid, v_vid, dy_vid = items
        d_attn = lax.dot_general(dy_vid, w_out, (((1,), (1,)), ((), ())), preferred_element_type=jnp.float32).astype(jnp.bfloat16)
        attn_b, grad_q, grad_k, grad_v = video_backward(q_vid, k_vid, v_vid, d_attn, block_index, block_count)
        term = lax.dot_general(attn_b, dy_vid, (((0,), (0,)), ((), ())), preferred_element_type=jnp.float32)
        return (total + term, (grad_q, grad_k, grad_v))
    start = jnp.zeros((HD, D), jnp.float32)
    total, grads = lax.scan(one_video, start, (query, key_states, value_states, grad_out))
    return (grads[0], grads[1], grads[2], total * TOKENS ** (-0.5))
```

```python
import functools

import jax
import jax.numpy as jnp
from jax import lax
from jax.experimental import pallas as pl
from jax.experimental.pallas import tpu as pltpu
from jax.sharding import PartitionSpec as P

HDIM = 64
BLK = 128
NT = (((1,), (1,)), ((), ()))
NN = (((1,), (0,)), ((), ()))
TN = (((0,), (0,)), ((), ()))
BF16 = jnp.bfloat16
F32 = jnp.float32


def join(a, b, head):
    cols = slice(head * HDIM, (head + 1) * HDIM)
    return jnp.concatenate([a[:, cols], b[:, cols]], axis=1)


def pack_kernel(a_ref, b_ref, out_ref):
    a, b = a_ref[...], b_ref[...]
    for peer in range(out_ref.shape[0]):
        for j in range(out_ref.shape[1]):
            out_ref[peer, j] = join(a, b, peer * out_ref.shape[1] + j)


def project_kernel(dy_ref, w_ref, q_ref, out_ref):
    d = lax.dot_general(dy_ref[...], w_ref[...], NT, preferred_element_type=F32).astype(BF16)
    q = q_ref[...]
    for peer in range(out_ref.shape[0]):
        for j in range(out_ref.shape[1]):
            out_ref[peer, j] = join(q, d, peer * out_ref.shape[1] + j)


def unpack_kernel(x_ref, a_ref, b_ref):
    peers, per, _, _ = x_ref.shape
    parts = [x_ref[p, j] for p in range(peers) for j in range(per)]
    a_ref[...] = jnp.concatenate([x[:, :HDIM] for x in parts], axis=1)
    b_ref[...] = jnp.concatenate([x[:, HDIM:] for x in parts], axis=1)


def weight_kernel(x_ref, dy_ref, a_ref, gw_ref):
    peers, per, _, _ = x_ref.shape
    parts = [x_ref[p, j] for p in range(peers) for j in range(per)]
    a_ref[...] = jnp.concatenate([x[:, :HDIM] for x in parts], axis=1)
    attn = jnp.concatenate([x[:, HDIM:] for x in parts], axis=1)
    gw_ref[...] = lax.dot_general(attn, dy_ref[...], TN, preferred_element_type=F32).astype(BF16)


def attn_block(n, h, i, idx_ref, qd_ref, kv_ref, kvt_ref, acc_ref, out_ref):
    per = qd_ref.shape[2] // BLK

    def rows(block):
        return pl.ds(pl.multiple_of(block * BLK, BLK), BLK)

    qd = qd_ref[i // per, h, rows(i % per), :]
    left = lax.broadcasted_iota(jnp.int32, (BLK, BLK), 1) < HDIM
    qs = jnp.where(left, qd * BF16(HDIM**-0.5), jnp.zeros_like(qd))
    do = jnp.where(left, jnp.zeros_like(qd), qd)
    both = jnp.concatenate([qs, do], axis=0)
    ids = [idx_ref[h, i, m] for m in range(n)]
    sd = [
        lax.dot_general(
            kv_ref[b // per, h, rows(b % per), :], both, NT, preferred_element_type=F32
        )
        for b in ids
    ]
    s = [x[:, :BLK] for x in sd]
    dp = [x[:, BLK:] for x in sd]
    top = jnp.max(functools.reduce(jnp.maximum, s), axis=0, keepdims=True)
    w = [jnp.exp(x - top) for x in s]
    inv = 1.0 / jnp.sum(functools.reduce(jnp.add, w), axis=0, keepdims=True)
    p = [x * inv for x in w]
    delta = jnp.sum(
        functools.reduce(jnp.add, [a * b for a, b in zip(p, dp)]), axis=0, keepdims=True
    )
    ds = [a * (b - delta) for a, b in zip(p, dp)]
    dsp = [jnp.concatenate([a.astype(BF16), b.astype(BF16)], axis=1) for a, b in zip(ds, p)]
    for m in range(n):
        acc_ref[h, rows(ids[m]), :] += lax.dot_general(
            dsp[m], both, NN, preferred_element_type=F32
        )
    kt = jnp.concatenate([kvt_ref[h, :, rows(b)] for b in ids], axis=1)
    o = lax.dot_general(kt, jnp.concatenate(dsp, axis=0), NN, preferred_element_type=F32)
    upper = lax.broadcasted_iota(jnp.int32, (BLK, BLK), 0) < HDIM
    res = jnp.where(upper, o[:, :BLK] * HDIM**-0.5, o[:, BLK:])
    out_ref[i // per, h, rows(i % per), :] = res.T.astype(BF16)


def attn_kernel(idx_ref, cnt_ref, qd_ref, kv_ref, out_ref, dkv_ref, kvt_ref, acc_ref):
    peers, heads, per, _ = qd_ref.shape
    per = per // BLK
    blocks = peers * per
    slots = idx_ref.shape[2]

    def rows(block):
        return pl.ds(pl.multiple_of(block * BLK, BLK), BLK)

    @pl.loop(0, heads)
    def _(h):
        @pl.loop(0, blocks)
        def _(j):
            kvt_ref[h, :, rows(j)] = kv_ref[j // per, h, rows(j % per), :].T
            acc_ref[h, rows(j), :] = jnp.zeros((BLK, BLK), F32)

        @pl.loop(0, blocks)
        def _(i):
            c = cnt_ref[h, i]
            for n in range(1, slots + 1):

                @pl.when(c == n)
                def _():
                    attn_block(n, h, i, idx_ref, qd_ref, kv_ref, kvt_ref, acc_ref, out_ref)

        @pl.loop(0, blocks)
        def _(j):
            dkv_ref[j // per, h, rows(j % per), :] = acc_ref[h, rows(j), :].astype(BF16)


V = pl.BlockSpec(memory_space=pltpu.VMEM)
S = pl.BlockSpec(memory_space=pltpu.SMEM)


def cost(flops, *arrays):
    return pl.CostEstimate(
        flops=flops, bytes_accessed=sum(a.size * a.dtype.itemsize for a in arrays), transcendentals=0
    )


def attention(idx, cnt, qd, kv):
    peers, heads, per, _ = qd.shape
    seq = peers * per
    out = jax.ShapeDtypeStruct(qd.shape, BF16)
    return pl.pallas_call(
        attn_kernel,
        out_shape=(out, out),
        in_specs=[S, S, V, V],
        out_specs=(V, V),
        scratch_shapes=[
            pltpu.VMEM((heads, BLK, seq), BF16),
            pltpu.VMEM((heads, seq, BLK), F32),
        ],
        compiler_params=pltpu.CompilerParams(vmem_limit_bytes=48 * 2**20),
        cost_estimate=cost(60_000_000_000, qd, kv, out, out),
        name="attention",
    )(idx, cnt, qd, kv)


def wide(rows, cols, pos=1):
    return pl.BlockSpec((rows, cols), (lambda t: (0, t)) if pos else (lambda t: (t, 0)))


def local(query, key_states, value_states, grad_out, w_out, block_index, block_count):
    rows, hd = query.shape[1:]
    depth = grad_out.shape[2]
    n_seq, n_dp = lax.axis_size("seq"), lax.axis_size("dp")
    heads = hd // HDIM
    per = heads // n_seq
    tiles = n_seq // 2
    cols = hd // tiles
    packed = jax.ShapeDtypeStruct((n_seq, per, rows, BLK), BF16)
    pairs = pl.BlockSpec((2, per, rows, BLK), lambda t: (t, 0, 0, 0))
    flat = jax.ShapeDtypeStruct((rows, hd), BF16)
    big = pltpu.CompilerParams(vmem_limit_bytes=48 * 2**20)
    q, k, v, dy = query[0], key_states[0], value_states[0], grad_out[0]

    def swap(x):
        return lax.all_to_all(x, "seq", split_axis=0, concat_axis=0, tiled=True)

    w_all = lax.all_gather(w_out, "dp", axis=0, tiled=True)
    kv = pl.pallas_call(
        pack_kernel, out_shape=packed, grid=(tiles,), in_specs=[wide(rows, cols)] * 2, out_specs=pairs,
        cost_estimate=cost(0, k, v, packed), name="pack",
    )(k, v)
    kv = swap(kv)
    qd = pl.pallas_call(
        project_kernel, out_shape=packed, grid=(tiles,),
        in_specs=[pl.BlockSpec((rows, depth), lambda t: (0, 0)), wide(cols, depth, 0), wide(rows, cols)],
        out_specs=pairs, compiler_params=big,
        cost_estimate=cost(2 * rows * depth * hd, dy, w_all, q, packed), name="project",
    )(dy, w_all, q)
    qd = swap(qd)
    first = lax.axis_index("seq") * per
    idx = lax.dynamic_slice_in_dim(block_index, first, per, 0)
    cnt = lax.dynamic_slice_in_dim(block_count, first, per, 0)
    odq, dkv = attention(idx, cnt, qd, kv)
    odq, dkv = swap(odq), swap(dkv)
    dq, gw = pl.pallas_call(
        weight_kernel, out_shape=(flat, jax.ShapeDtypeStruct((hd, depth), BF16)), grid=(tiles,),
        in_specs=[pairs, pl.BlockSpec((rows, depth), lambda t: (0, 0))],
        out_specs=(wide(rows, cols), wide(cols, depth, 0)), compiler_params=big,
        cost_estimate=cost(2 * rows * depth * hd, dy, w_all, packed), name="weight",
    )(odq, dy)
    dk, dv = pl.pallas_call(
        unpack_kernel, out_shape=(flat, flat), grid=(tiles,), in_specs=[pairs],
        out_specs=(wide(rows, cols),) * 2, cost_estimate=cost(0, k, v, packed), name="unpack",
    )(dkv)
    gw = lax.psum_scatter(gw.reshape(n_seq, hd // n_seq, depth), "seq", scatter_dimension=0)
    gw = lax.psum_scatter(
        gw.reshape(n_dp, hd // n_seq // n_dp, depth), "dp", scatter_dimension=0
    )
    scale = float(rows * n_seq * n_dp) ** (-0.5)
    return dq[None], dk[None], dv[None], gw.astype(F32) * scale


def solution(mesh):
    tok = P("dp", "seq", None)
    return jax.shard_map(
        local,
        mesh=mesh,
        in_specs=(tok, tok, tok, tok, P("dp", None), P(), P()),
        out_specs=(tok, tok, tok, P(("seq", "dp"), None)),
        check_vma=False,
    )
```

```python
import functools

import jax
import jax.numpy as jnp
from jax import lax
from jax.experimental import pallas as pl
from jax.experimental.pallas import tpu as pltpu
from jax.sharding import PartitionSpec as P

HDIM = 64
BLK = 128
NT = (((1,), (1,)), ((), ()))
NN = (((1,), (0,)), ((), ()))
TN = (((0,), (0,)), ((), ()))
BF16 = jnp.bfloat16
F32 = jnp.float32
MESH = pl.DeviceIdType.MESH
TB = 3
Q_AT = 1152


def pack_kernel(q_ref, k_ref, v_ref, out_ref):
    k, v = k_ref[...], v_ref[...]
    rows = k.shape[0]
    qt = q_ref[...].T
    feats = qt.shape[0] // 2
    for peer in range(2):
        for j in range(feats // HDIM):
            cols = slice(peer * feats + j * HDIM, peer * feats + (j + 1) * HDIM)
            out_ref[peer, j * rows : (j + 1) * rows] = jnp.concatenate([k[:, cols], v[:, cols]], axis=1)
        for t in range(rows // BLK):
            at = Q_AT + t * feats
            out_ref[peer, at : at + feats] = qt[peer * feats : (peer + 1) * feats, t * BLK : (t + 1) * BLK]


def project_kernel(dy_ref, w_ref, out_ref):
    d = lax.dot_general(w_ref[...], dy_ref[...], NT, preferred_element_type=F32).astype(BF16)
    feats = d.shape[0] // 2
    for peer in range(2):
        for t in range(d.shape[1] // BLK):
            out_ref[peer, t * feats : (t + 1) * feats] = d[
                peer * feats : (peer + 1) * feats, t * BLK : (t + 1) * BLK
            ]


def unpack_kernel(x_ref, q_ref, k_ref, v_ref):
    rows = q_ref.shape[0]
    feats = q_ref.shape[1] // 2
    ks, vs, qs = [], [], []
    for peer in range(2):
        for j in range(feats // HDIM):
            x = x_ref[peer, j * rows : (j + 1) * rows]
            ks.append(x[:, :HDIM])
            vs.append(x[:, HDIM:])
        qs.append(
            jnp.concatenate(
                [x_ref[peer, Q_AT + t * feats : Q_AT + (t + 1) * feats] for t in range(rows // BLK)], axis=1
            )
        )
    q_ref[...] = jnp.concatenate(qs, axis=0).T
    k_ref[...] = jnp.concatenate(ks, axis=1)
    v_ref[...] = jnp.concatenate(vs, axis=1)


def attn_block(n, h, i, idx_ref, x_ref, d_ref, kvt_ref, acc_ref, at_ref, g_ref):
    tb = TB
    feats = d_ref.shape[1] // tb
    per = tb * BLK

    def key_rows(b):
        return pl.ds(pl.multiple_of(h * per + (b % tb) * BLK, BLK), BLK)

    def seq_rows(b):
        return pl.ds(pl.multiple_of(b * BLK, BLK), BLK)

    at = pl.multiple_of((i % tb) * feats + h * HDIM, HDIM)
    qt = x_ref[i // tb, pl.ds(pl.multiple_of(Q_AT + at, HDIM), HDIM), :] * BF16(HDIM**-0.5)
    dt = d_ref[i // tb, pl.ds(at, HDIM), :]
    zero = jnp.zeros_like(qt)
    both = jnp.concatenate(
        [jnp.concatenate([qt, zero], axis=1), jnp.concatenate([zero, dt], axis=1)], axis=0
    )
    ids = [idx_ref[h, i, m] for m in range(n)]
    sd = [
        lax.dot_general(x_ref[b // tb, key_rows(b), :], both, NN, preferred_element_type=F32)
        for b in ids
    ]
    s = [x[:, :BLK] for x in sd]
    dp = [x[:, BLK:] for x in sd]
    top = jnp.max(functools.reduce(jnp.maximum, s), axis=0, keepdims=True)
    w = [jnp.exp(x - top) for x in s]
    inv = 1.0 / jnp.sum(functools.reduce(jnp.add, w), axis=0, keepdims=True)
    p = [x * inv for x in w]
    delta = jnp.sum(
        functools.reduce(jnp.add, [a * b for a, b in zip(p, dp)]), axis=0, keepdims=True
    )
    ds = [a * (b - delta) for a, b in zip(p, dp)]
    dsp = [jnp.concatenate([a.astype(BF16), b.astype(BF16)], axis=1) for a, b in zip(ds, p)]
    for m in range(n):
        acc_ref[h, seq_rows(ids[m]), :] += lax.dot_general(
            dsp[m], both, NT, preferred_element_type=F32
        )
    kt = jnp.concatenate([kvt_ref[h, :, seq_rows(b)] for b in ids], axis=1)
    o = lax.dot_general(kt, jnp.concatenate(dsp, axis=0), NN, preferred_element_type=F32)
    g_ref[i // tb, pl.ds(pl.multiple_of(Q_AT + at, HDIM), HDIM), :] = (
        o[:HDIM, :BLK] * HDIM**-0.5
    ).astype(BF16)
    at_ref[i // tb, pl.ds(at, HDIM), :] = o[HDIM:, BLK:].astype(BF16)


def attn_kernel(idx_ref, cnt_ref, x_ref, d_ref, at_ref, g_ref, kvt_ref, acc_ref):
    heads, blocks = cnt_ref.shape
    tb = blocks // x_ref.shape[0]
    slots = idx_ref.shape[2]

    def key_rows(h, b):
        return pl.ds(pl.multiple_of(h * tb * BLK + (b % tb) * BLK, BLK), BLK)

    def seq_rows(b):
        return pl.ds(pl.multiple_of(b * BLK, BLK), BLK)

    @pl.loop(0, heads)
    def _(h):
        @pl.loop(0, blocks)
        def _(j):
            kvt_ref[h, :, seq_rows(j)] = x_ref[j // tb, key_rows(h, j), :].T
            acc_ref[h, seq_rows(j), :] = jnp.zeros((BLK, BLK), F32)

        @pl.loop(0, blocks)
        def _(i):
            c = cnt_ref[h, i]
            for n in range(1, slots + 1):

                @pl.when(c == n)
                def _():
                    attn_block(n, h, i, idx_ref, x_ref, d_ref, kvt_ref, acc_ref, at_ref, g_ref)

        @pl.loop(0, blocks)
        def _(j):
            g_ref[j // tb, key_rows(h, j), :] = acc_ref[h, seq_rows(j), :].astype(BF16)


def back_kernel(scale, at_ref, g_ref, dy_ref, gr_ref, gw_ref, atr, dyx, part, ring, plane, total, half, other,
                at_s, at_r, fw_s, fw_r, dy_s, dy_r, g_s, g_r, z_s, z_r, p_s, p_r, o_s, o_r, loc):
    dp, me = lax.axis_index("dp"), lax.axis_index("seq")
    core, zz, lo = dp % 2, (dp // 2) % 4, dp // 8
    sib = dp + 1 - 2 * core
    tiles, nz, slabs, srows, tcols = part.shape
    peers = at_ref.shape[0]
    feats = at_ref.shape[1] // TB
    tb = TB
    cols = dyx.shape[2]
    my = me * 2 + lo

    def at_z(k):
        return lo * 8 + lax.rem(zz + k + nz, nz) * 2 + core

    def plane_peer(k):
        j = lax.rem(my + k, slabs)
        return j, {"dp": (j % 2) * 8 + zz * 2 + core, "seq": j // 2}

    bar = pltpu.get_barrier_semaphore()

    def hello(where):
        pl.semaphore_signal(bar, inc=1, device_id=where, device_id_type=MESH)

    @pl.loop(1, slabs)
    def _(k):
        hello(plane_peer(k)[1])

    hello({"dp": sib})
    hello({"dp": at_z(1)})
    hello({"dp": at_z(-1)})
    pl.semaphore_wait(bar, slabs + 2)

    def remote(src, dst, ssem, rsem, where):
        return pltpu.make_async_remote_copy(
            src_ref=src, dst_ref=dst, send_sem=ssem, recv_sem=rsem, device_id=where, device_id_type=MESH
        )

    def at_copy(k):
        p = lax.rem(me + k, peers)
        return remote(at_ref.at[p], atr.at[0, me], at_s.at[k], at_r.at[k], {"seq": p})

    @pl.loop(1, peers)
    def _(k):
        at_copy(k).start()

    mine = pl.ds(pl.multiple_of(core * cols, BLK), cols)
    theirs = pl.ds(pl.multiple_of((1 - core) * cols, BLK), cols)
    dy_copy = remote(dy_ref.at[:, theirs], dyx.at[1], dy_s, dy_r, {"dp": sib})
    dy_copy.start()
    own_dy = pltpu.make_async_copy(dy_ref.at[:, mine], dyx.at[0], loc.at[0])
    own_dy.start()
    own_at = pltpu.make_async_copy(at_ref.at[me], atr.at[0, me], loc.at[1])
    own_at.start()
    own_g = pltpu.make_async_copy(g_ref.at[me], gr_ref.at[me], loc.at[2])
    own_g.start()

    def forward(s, k):
        return remote(atr.at[0, s], atr.at[1, s], fw_s.at[k], fw_r.at[k], {"dp": sib})

    own_at.wait()
    forward(me, 0).start()

    @pl.loop(1, peers)
    def _(k):
        at_copy(k).wait_recv()
        forward(lax.rem(me - k + peers, peers), k).start()

    def g_copy(k):
        p = lax.rem(me + k, peers)
        return remote(g_ref.at[p], gr_ref.at[me], g_s.at[k], g_r.at[k], {"seq": p})

    @pl.loop(1, peers)
    def _(k):
        g_copy(k).start()

    @pl.loop(0, peers)
    def _(k):
        forward(lax.rem(me - k + peers, peers), k).wait_recv()

    dy_copy.wait_recv()
    own_dy.wait()

    way = tiles // 2

    def z_copy(t, step):
        up = 1 if t < way else -1
        chunk = lax.rem(zz - up * (1 + step) + 2 * nz, nz)
        return chunk, remote(
            part.at[t, chunk], ring.at[t, step], z_s.at[t, step], z_r.at[t, step], {"dp": at_z(up)}
        )

    order = [t + w for t in range(way) for w in (0, way)]
    for t in order:
        tc = slice(t * tcols, (t + 1) * tcols)

        @pl.loop(0, peers)
        def _(s):
            lhs = jnp.concatenate(
                [atr[q, s, b * feats : (b + 1) * feats, :] for q in range(2) for b in range(tb)], axis=1
            )
            rhs = jnp.concatenate([dyx[q, :, tc] for q in range(2)], axis=0)
            prod = lax.dot_general(lhs, rhs, NN, preferred_element_type=F32)
            for j in range(2):
                for z in range(nz):
                    r = (j * nz + z) * srows
                    part[t, z, s * 2 + j] = prod[r : r + srows].astype(BF16)

        z_copy(t, 0)[1].start()

    for step in range(nz - 1):
        for t in order:
            z_copy(t, step)[1].wait_recv()
            up = 1 if t < way else -1
            chunk = lax.rem(zz - up * (2 + step) + 2 * nz, nz)
            part[t, chunk] = (part[t, chunk].astype(F32) + ring[t, step].astype(F32)).astype(BF16)
            if step < nz - 2:
                z_copy(t, step + 1)[1].start()

    def p_copy(k):
        j, where = plane_peer(k)
        return remote(part.at[:, zz, j], plane.at[k], p_s.at[k], p_r.at[k], where)

    @pl.loop(1, slabs)
    def _(k):
        p_copy(k).start()

    total[...] = part[:, zz, my].astype(F32)

    @pl.loop(1, slabs)
    def _(k):
        p_copy(k).wait_recv()
        total[...] += plane[k].astype(F32)

    rows = gw_ref.shape[0]
    for c in range(2):
        half[c] = total[:, c * rows : (c + 1) * rows, :] * scale
    swap = remote(half.at[1 - core], other, o_s, o_r, {"dp": sib})
    swap.start()
    swap.wait_recv()
    for t in range(tiles):
        gw_ref[:, pl.ds(pl.multiple_of(core * cols + t * tcols, BLK), tcols)] = half[core, t]
        gw_ref[:, pl.ds(pl.multiple_of((1 - core) * cols + t * tcols, BLK), tcols)] = other[t]

    swap.wait_send()
    dy_copy.wait_send()
    own_g.wait()
    forward(me, 0).wait_send()

    @pl.loop(1, peers)
    def _(k):
        at_copy(k).wait_send()
        forward(lax.rem(me - k + peers, peers), k).wait_send()
        g_copy(k).wait()

    for step in range(nz - 1):
        for t in order:
            z_copy(t, step)[1].wait_send()

    @pl.loop(1, slabs)
    def _(k):
        p_copy(k).wait_send()


def bring_back(at, g, dy, scale):
    peers = at.shape[0]
    rows, depth = dy.shape
    tiles, tcols, nz, slabs = 6, 256, 4, 16
    out_rows = peers * 192 // 128
    dma = pltpu.SemaphoreType.DMA
    return pl.pallas_call(
        functools.partial(back_kernel, scale),
        out_shape=(jax.ShapeDtypeStruct(g.shape, BF16), jax.ShapeDtypeStruct((out_rows, depth), F32)),
        in_specs=[V, V, V],
        out_specs=(V, V),
        scratch_shapes=[
            pltpu.VMEM((2, *at.shape), BF16),
            pltpu.VMEM((2, rows, depth // 2), BF16),
            pltpu.VMEM((tiles, nz, slabs, 2 * out_rows, tcols), BF16),
            pltpu.VMEM((tiles, nz - 1, slabs, 2 * out_rows, tcols), BF16),
            pltpu.VMEM((slabs, tiles, 2 * out_rows, tcols), BF16),
            pltpu.VMEM((tiles, 2 * out_rows, tcols), F32),
            pltpu.VMEM((2, tiles, out_rows, tcols), F32),
            pltpu.VMEM((tiles, out_rows, tcols), F32),
            dma((peers,)), dma((peers,)), dma((peers,)), dma((peers,)), dma, dma,
            dma((peers,)), dma((peers,)), dma((tiles, nz - 1)), dma((tiles, nz - 1)),
            dma((slabs,)), dma((slabs,)), dma, dma, dma((3,)),
        ],
        compiler_params=pltpu.CompilerParams(
            collective_id=1, has_side_effects=True, vmem_limit_bytes=56 * 2**20
        ),
        cost_estimate=cost(2 * rows * depth * peers * 192, at, g, g, dy),
        name="bring_back",
    )(at, g, dy)


V = pl.BlockSpec(memory_space=pltpu.VMEM)
S = pl.BlockSpec(memory_space=pltpu.SMEM)


def cost(flops, *arrays):
    return pl.CostEstimate(
        flops=flops, bytes_accessed=sum(a.size * a.dtype.itemsize for a in arrays), transcendentals=0
    )


def attention(idx, cnt, x, d):
    heads, blocks = cnt.shape
    seq = blocks * BLK
    return pl.pallas_call(
        attn_kernel,
        out_shape=(jax.ShapeDtypeStruct(d.shape, BF16), jax.ShapeDtypeStruct(x.shape, BF16)),
        in_specs=[S, S, V, V],
        out_specs=(V, V),
        scratch_shapes=[
            pltpu.VMEM((heads, BLK, seq), BF16),
            pltpu.VMEM((heads, seq, BLK), F32),
        ],
        compiler_params=pltpu.CompilerParams(vmem_limit_bytes=48 * 2**20),
        cost_estimate=cost(60_000_000_000, x, d, x, d),
        name="attention",
    )(idx, cnt, x, d)


def wide(rows, cols, pos=1):
    return pl.BlockSpec((rows, cols), (lambda t: (0, t)) if pos else (lambda t: (t, 0)))


def local(query, key_states, value_states, grad_out, w_out, block_index, block_count):
    rows, hd = query.shape[1:]
    depth = grad_out.shape[2]
    n_seq, n_dp = lax.axis_size("seq"), lax.axis_size("dp")
    per = hd // HDIM // n_seq
    tiles = n_seq // 2
    cols = hd // tiles
    x_rows = per * rows + TB * per * HDIM
    d_rows = TB * per * HDIM
    packed = jax.ShapeDtypeStruct((n_seq, x_rows, BLK), BF16)
    small = jax.ShapeDtypeStruct((n_seq, d_rows, BLK), BF16)
    pairs = pl.BlockSpec((2, x_rows, BLK), lambda t: (t, 0, 0))
    pairs_d = pl.BlockSpec((2, d_rows, BLK), lambda t: (t, 0, 0))
    flat = jax.ShapeDtypeStruct((rows, hd), BF16)
    big = pltpu.CompilerParams(vmem_limit_bytes=48 * 2**20)
    q, k, v, dy = query[0], key_states[0], value_states[0], grad_out[0]

    def swap(x):
        return lax.all_to_all(x, "seq", split_axis=0, concat_axis=0, tiled=True)

    w_all = lax.all_gather(w_out, "dp", axis=0, tiled=True)
    x = pl.pallas_call(
        pack_kernel, out_shape=packed, grid=(tiles,), in_specs=[wide(rows, cols)] * 3, out_specs=pairs,
        cost_estimate=cost(0, q, k, v, packed), name="pack",
    )(q, k, v)
    x = swap(x)
    d = pl.pallas_call(
        project_kernel, out_shape=small, grid=(tiles,),
        in_specs=[pl.BlockSpec((rows, depth), lambda t: (0, 0)), wide(cols, depth, 0)],
        out_specs=pairs_d, compiler_params=big,
        cost_estimate=cost(2 * rows * depth * hd, dy, w_all, small), name="project",
    )(dy, w_all)
    d = swap(d)
    first = lax.axis_index("seq") * per
    idx = lax.dynamic_slice_in_dim(block_index, first, per, 0)
    cnt = lax.dynamic_slice_in_dim(block_count, first, per, 0)
    at, g = attention(idx, cnt, x, d)
    scale = float(rows * n_seq * n_dp) ** (-0.5)
    gr, gw = bring_back(at, g, dy, scale)
    dq, dk, dv = pl.pallas_call(
        unpack_kernel, out_shape=(flat,) * 3, grid=(tiles,), in_specs=[pairs],
        out_specs=(wide(rows, cols),) * 3, cost_estimate=cost(0, q, k, v, packed), name="unpack",
    )(gr)
    return dq[None], dk[None], dv[None], gw


def solution(mesh):
    tok = P("dp", "seq", None)
    return jax.shard_map(
        local,
        mesh=mesh,
        in_specs=(tok, tok, tok, tok, P("dp", None), P(), P()),
        out_specs=(tok, tok, tok, P(("seq", "dp"), None)),
        check_vma=False,
    )
```

```python
import functools

import jax
import jax.numpy as jnp
from jax import lax
from jax.experimental import pallas as pl
from jax.experimental.pallas import tpu as pltpu
from jax.sharding import PartitionSpec as P

HDIM = 64
BLK = 128
NT = (((1,), (1,)), ((), ()))
NN = (((1,), (0,)), ((), ()))
TN = (((0,), (0,)), ((), ()))
BF16 = jnp.bfloat16
F32 = jnp.float32
MESH = pl.DeviceIdType.MESH
TB = 3
Q_AT = 1152


def front_kernel(q_ref, k_ref, v_ref, dy_ref, w_ref, xr_ref, dr_ref, xs, ds, wall,
                 x_s, x_r, d_s, d_r, z_s, z_r, y_s, y_r, f_s, f_r, loc):
    dp, me = lax.axis_index("dp"), lax.axis_index("seq")
    core, zz, lo = dp % 2, (dp // 2) % 4, dp // 8
    sib, mate = dp + 1 - 2 * core, dp + 8 - 16 * lo
    peers, nz = xs.shape[0], wall.shape[2]
    rows = q_ref.shape[0]
    feats = q_ref.shape[1] // peers
    part = wall.shape[3] // 2

    def at_z(k):
        return lo * 8 + lax.rem(zz + k + nz, nz) * 2 + core

    bar = pltpu.get_barrier_semaphore()

    def hello(where):
        pl.semaphore_signal(bar, inc=1, device_id=where, device_id_type=MESH)

    @pl.loop(1, peers)
    def _(k):
        hello({"seq": lax.rem(me + k, peers)})

    for where in (sib, mate, at_z(1), at_z(-1)):
        hello({"dp": where})
    pl.semaphore_wait(bar, peers + 3)

    def remote(src, dst, ssem, rsem, where):
        return pltpu.make_async_remote_copy(
            src_ref=src, dst_ref=dst, send_sem=ssem, recv_sem=rsem, device_id=where, device_id_type=MESH
        )

    def row(l):
        return lo if l == 0 else 1 - lo

    def cell(l, k, c=None):
        return wall.at[core if c is None else c, row(l), lax.rem(zz - k + nz, nz)]

    def source(l):
        return w_ref if l == 0 else cell(l, 0)

    def hop(l, up):
        d = 0 if up == 1 else 1
        return remote(source(l), cell(l, 0), z_s.at[l, d, 0], z_r.at[l, d, 0], {"dp": at_z(up)})

    def hop_in(l, up):
        d = 0 if up == 1 else 1
        return remote(cell(l, up), cell(l, up), z_s.at[l, d, 0], z_r.at[l, d, 0], {"dp": at_z(up)})

    def relay(l, up):
        d = 0 if up == 1 else 1
        h = pl.ds(d * part, part)
        c = cell(l, up).at[h]
        return remote(c, c, z_s.at[l, d, 1], z_r.at[l, d, 1], {"dp": at_z(up)})

    def relay_in(l, up):
        d = 0 if up == 1 else 1
        h = pl.ds(d * part, part)
        c = cell(l, 2).at[h]
        return remote(c, c, z_s.at[l, d, 1], z_r.at[l, d, 1], {"dp": at_z(up)})

    def over(l, k):
        return remote(
            w_ref if (l, k) == (0, 0) else cell(l, k), cell(l, k), f_s.at[l, k], f_r.at[l, k], {"dp": sib}
        )

    def over_in(l, k):
        c = cell(l, k, 1 - core)
        return remote(c, c, f_s.at[l, k], f_r.at[l, k], {"dp": sib})

    hop(0, 1).start()
    hop(0, -1).start()
    to_mate = remote(w_ref, cell(0, 0), y_s, y_r, {"dp": mate})
    to_mate.start()
    over(0, 0).start()
    own_w = pltpu.make_async_copy(w_ref, cell(0, 0), loc.at[0])
    own_w.start()

    k, v = k_ref[...], v_ref[...]
    for p in range(peers):
        for j in range(feats // HDIM):
            cols = slice(p * feats + j * HDIM, p * feats + (j + 1) * HDIM)
            xs[p, j * rows : (j + 1) * rows] = jnp.concatenate([k[:, cols], v[:, cols]], axis=1)
    for p in range(0, peers, 2):
        qt = q_ref[:, p * feats : (p + 2) * feats].T
        for i in range(2):
            for t in range(TB):
                at = Q_AT + t * feats
                xs[p + i, at : at + feats] = qt[i * feats : (i + 1) * feats, t * BLK : (t + 1) * BLK]

    def x_copy(k):
        p = lax.rem(me + k, peers)
        return remote(xs.at[p], xr_ref.at[me], x_s.at[k], x_r.at[k], {"seq": p})

    @pl.loop(1, peers)
    def _(k):
        x_copy(k).start()

    own_x = pltpu.make_async_copy(xs.at[me], xr_ref.at[me], loc.at[1])
    own_x.start()
    own_w.wait()

    def d_copy(n, s):
        return remote(ds.at[s], dr_ref.at[me], d_s.at[n], d_r.at[me], {"seq": s})

    def own_d():
        return pltpu.make_async_copy(ds.at[me], dr_ref.at[me], loc.at[2])

    def peer(l, k):
        return row(l) * nz + lax.rem(zz - k + nz, nz)

    def project(n, l, k):
        over_in(l, k).wait_recv()
        s, z = peer(l, k), lax.rem(zz - k + nz, nz)
        w2 = jnp.concatenate([wall[0, row(l), z], wall[1, row(l), z]], axis=0)
        d = lax.dot_general(w2, dy_ref[...], NT, preferred_element_type=F32).astype(BF16)
        for t in range(TB):
            ds[s, t * feats : (t + 1) * feats] = d[:, t * BLK : (t + 1) * BLK]

        @pl.when(s != me)
        def _():
            d_copy(n, s).start()

        @pl.when(s == me)
        def _():
            own_d().start()

    order = [(0, 0), (1, 0), (0, 1), (0, 3), (1, 1), (1, 3), (0, 2), (1, 2)]

    def spread(l):
        hop_in(l, 1).wait_recv()
        relay(l, 1).start()
        over(l, 1).start()
        hop_in(l, -1).wait_recv()
        relay(l, -1).start()
        over(l, 3).start()

    def finish(l):
        relay_in(l, 1).wait_recv()
        relay_in(l, -1).wait_recv()
        over(l, 2).start()

    project(0, *order[0])
    remote(cell(1, 0), cell(1, 0), y_s, y_r, {"dp": mate}).wait_recv()
    hop(1, 1).start()
    hop(1, -1).start()
    over(1, 0).start()
    spread(0)
    project(1, *order[1])
    project(2, *order[2])
    project(3, *order[3])
    spread(1)
    project(4, *order[4])
    project(5, *order[5])
    finish(0)
    project(6, *order[6])
    finish(1)
    project(7, *order[7])

    for l in range(2):
        for up in (1, -1):
            hop(l, up).wait_send()
            relay(l, up).wait_send()
        for k in range(nz):
            over(l, k).wait_send()
    to_mate.wait_send()
    own_x.wait()

    @pl.loop(1, peers)
    def _(k):
        x_copy(k).wait()

    for n, (l, k) in enumerate(order):
        s = peer(l, k)

        @pl.when(s != me)
        def _():
            d_copy(n, s).wait_send()

        @pl.when(s == me)
        def _():
            own_d().wait()

    @pl.loop(1, peers)
    def _(k):
        p = lax.rem(me + k, peers)
        remote(ds.at[p], dr_ref.at[p], d_s.at[0], d_r.at[p], {"seq": p}).wait_recv()


def unpack_kernel(x_ref, q_ref, k_ref, v_ref):
    rows = q_ref.shape[0]
    feats = q_ref.shape[1] // 2
    ks, vs, qs = [], [], []
    for peer in range(2):
        for j in range(feats // HDIM):
            x = x_ref[peer, j * rows : (j + 1) * rows]
            ks.append(x[:, :HDIM])
            vs.append(x[:, HDIM:])
        qs.append(
            jnp.concatenate(
                [x_ref[peer, Q_AT + t * feats : Q_AT + (t + 1) * feats] for t in range(rows // BLK)], axis=1
            )
        )
    q_ref[...] = jnp.concatenate(qs, axis=0).T
    k_ref[...] = jnp.concatenate(ks, axis=1)
    v_ref[...] = jnp.concatenate(vs, axis=1)


def attn_block(n, h, i, idx_ref, x_ref, d_ref, kvt_ref, acc_ref, at_ref, g_ref):
    tb = TB
    feats = d_ref.shape[1] // tb
    per = tb * BLK

    def key_rows(b):
        return pl.ds(pl.multiple_of(h * per + (b % tb) * BLK, BLK), BLK)

    def seq_rows(b):
        return pl.ds(pl.multiple_of(b * BLK, BLK), BLK)

    at = pl.multiple_of((i % tb) * feats + h * HDIM, HDIM)
    qt = x_ref[i // tb, pl.ds(pl.multiple_of(Q_AT + at, HDIM), HDIM), :] * BF16(HDIM**-0.5)
    dt = d_ref[i // tb, pl.ds(at, HDIM), :]
    zero = jnp.zeros_like(qt)
    both = jnp.concatenate(
        [jnp.concatenate([qt, zero], axis=1), jnp.concatenate([zero, dt], axis=1)], axis=0
    )
    ids = [idx_ref[h, i, m] for m in range(n)]
    sd = [
        lax.dot_general(x_ref[b // tb, key_rows(b), :], both, NN, preferred_element_type=F32)
        for b in ids
    ]
    s = [x[:, :BLK] for x in sd]
    dp = [x[:, BLK:] for x in sd]
    top = jnp.max(functools.reduce(jnp.maximum, s), axis=0, keepdims=True)
    w = [jnp.exp(x - top) for x in s]
    inv = 1.0 / jnp.sum(functools.reduce(jnp.add, w), axis=0, keepdims=True)
    p = [x * inv for x in w]
    delta = jnp.sum(
        functools.reduce(jnp.add, [a * b for a, b in zip(p, dp)]), axis=0, keepdims=True
    )
    ds = [a * (b - delta) for a, b in zip(p, dp)]
    dsp = [jnp.concatenate([a.astype(BF16), b.astype(BF16)], axis=1) for a, b in zip(ds, p)]
    for m in range(n):
        acc_ref[h, seq_rows(ids[m]), :] += lax.dot_general(
            dsp[m], both, NT, preferred_element_type=F32
        )
    kt = jnp.concatenate([kvt_ref[h, :, seq_rows(b)] for b in ids], axis=1)
    o = lax.dot_general(kt, jnp.concatenate(dsp, axis=0), NN, preferred_element_type=F32)
    g_ref[i // tb, pl.ds(pl.multiple_of(Q_AT + at, HDIM), HDIM), :] = (
        o[:HDIM, :BLK] * HDIM**-0.5
    ).astype(BF16)
    at_ref[i // tb, pl.ds(at, HDIM), :] = o[HDIM:, BLK:].astype(BF16)


def attn_kernel(idx_ref, cnt_ref, x_ref, d_ref, at_ref, g_ref, kvt_ref, acc_ref):
    heads, blocks = cnt_ref.shape
    tb = blocks // x_ref.shape[0]
    slots = idx_ref.shape[2]

    def key_rows(h, b):
        return pl.ds(pl.multiple_of(h * tb * BLK + (b % tb) * BLK, BLK), BLK)

    def seq_rows(b):
        return pl.ds(pl.multiple_of(b * BLK, BLK), BLK)

    @pl.loop(0, heads)
    def _(h):
        @pl.loop(0, blocks)
        def _(j):
            kvt_ref[h, :, seq_rows(j)] = x_ref[j // tb, key_rows(h, j), :].T
            acc_ref[h, seq_rows(j), :] = jnp.zeros((BLK, BLK), F32)

        @pl.loop(0, blocks)
        def _(i):
            c = cnt_ref[h, i]
            for n in range(1, slots + 1):

                @pl.when(c == n)
                def _():
                    attn_block(n, h, i, idx_ref, x_ref, d_ref, kvt_ref, acc_ref, at_ref, g_ref)

        @pl.loop(0, blocks)
        def _(j):
            g_ref[j // tb, key_rows(h, j), :] = acc_ref[h, seq_rows(j), :].astype(BF16)


def back_kernel(scale, at_ref, g_ref, dy_ref, gr_ref, gw_ref, atr, dyx, part, ring, plane, total, half, other,
                at_s, at_r, fw_s, fw_r, dy_s, dy_r, g_s, g_r, z_s, z_r, p_s, p_r, o_s, o_r, loc):
    dp, me = lax.axis_index("dp"), lax.axis_index("seq")
    core, zz, lo = dp % 2, (dp // 2) % 4, dp // 8
    sib = dp + 1 - 2 * core
    tiles, nz, slabs, srows, tcols = part.shape
    peers = at_ref.shape[0]
    feats = at_ref.shape[1] // TB
    tb = TB
    cols = dyx.shape[2]
    my = me * 2 + lo

    def at_z(k):
        return lo * 8 + lax.rem(zz + k + nz, nz) * 2 + core

    def plane_peer(k):
        j = lax.rem(my + k, slabs)
        return j, {"dp": (j % 2) * 8 + zz * 2 + core, "seq": j // 2}

    bar = pltpu.get_barrier_semaphore()

    def hello(where):
        pl.semaphore_signal(bar, inc=1, device_id=where, device_id_type=MESH)

    @pl.loop(1, slabs)
    def _(k):
        hello(plane_peer(k)[1])

    hello({"dp": sib})
    hello({"dp": at_z(1)})
    hello({"dp": at_z(-1)})
    pl.semaphore_wait(bar, slabs + 2)

    def remote(src, dst, ssem, rsem, where):
        return pltpu.make_async_remote_copy(
            src_ref=src, dst_ref=dst, send_sem=ssem, recv_sem=rsem, device_id=where, device_id_type=MESH
        )

    def at_copy(k):
        p = lax.rem(me + k, peers)
        return remote(at_ref.at[p], atr.at[0, me], at_s.at[k], at_r.at[k], {"seq": p})

    @pl.loop(1, peers)
    def _(k):
        at_copy(k).start()

    mine = pl.ds(pl.multiple_of(core * cols, BLK), cols)
    theirs = pl.ds(pl.multiple_of((1 - core) * cols, BLK), cols)
    dy_copy = remote(dy_ref.at[:, theirs], dyx.at[1], dy_s, dy_r, {"dp": sib})
    dy_copy.start()
    own_dy = pltpu.make_async_copy(dy_ref.at[:, mine], dyx.at[0], loc.at[0])
    own_dy.start()
    own_at = pltpu.make_async_copy(at_ref.at[me], atr.at[0, me], loc.at[1])
    own_at.start()
    own_g = pltpu.make_async_copy(g_ref.at[me], gr_ref.at[me], loc.at[2])
    own_g.start()

    def forward(s, k):
        return remote(atr.at[0, s], atr.at[1, s], fw_s.at[k], fw_r.at[k], {"dp": sib})

    own_at.wait()
    forward(me, 0).start()

    @pl.loop(1, peers)
    def _(k):
        at_copy(k).wait_recv()
        forward(lax.rem(me - k + peers, peers), k).start()

    def g_copy(k):
        p = lax.rem(me + k, peers)
        return remote(g_ref.at[p], gr_ref.at[me], g_s.at[k], g_r.at[k], {"seq": p})

    @pl.loop(1, peers)
    def _(k):
        g_copy(k).start()

    @pl.loop(0, peers)
    def _(k):
        forward(lax.rem(me - k + peers, peers), k).wait_recv()

    dy_copy.wait_recv()
    own_dy.wait()

    way = tiles // 2

    def z_copy(t, step):
        up = 1 if t < way else -1
        chunk = lax.rem(zz - up * (1 + step) + 2 * nz, nz)
        return chunk, remote(
            part.at[t, chunk], ring.at[t, step], z_s.at[t, step], z_r.at[t, step], {"dp": at_z(up)}
        )

    order = [t + w for t in range(way) for w in (0, way)]
    for t in order:
        tc = slice(t * tcols, (t + 1) * tcols)

        @pl.loop(0, peers)
        def _(s):
            lhs = jnp.concatenate(
                [atr[q, s, b * feats : (b + 1) * feats, :] for q in range(2) for b in range(tb)], axis=1
            )
            rhs = jnp.concatenate([dyx[q, :, tc] for q in range(2)], axis=0)
            prod = lax.dot_general(lhs, rhs, NN, preferred_element_type=F32)
            for j in range(2):
                for z in range(nz):
                    r = (j * nz + z) * srows
                    part[t, z, s * 2 + j] = prod[r : r + srows].astype(BF16)

        z_copy(t, 0)[1].start()

    for step in range(nz - 1):
        for t in order:
            z_copy(t, step)[1].wait_recv()
            up = 1 if t < way else -1
            chunk = lax.rem(zz - up * (2 + step) + 2 * nz, nz)
            part[t, chunk] = (part[t, chunk].astype(F32) + ring[t, step].astype(F32)).astype(BF16)
            if step < nz - 2:
                z_copy(t, step + 1)[1].start()

    def p_copy(k):
        j, where = plane_peer(k)
        return remote(part.at[:, zz, j], plane.at[k], p_s.at[k], p_r.at[k], where)

    @pl.loop(1, slabs)
    def _(k):
        p_copy(k).start()

    total[...] = part[:, zz, my].astype(F32)

    @pl.loop(1, slabs)
    def _(k):
        p_copy(k).wait_recv()
        total[...] += plane[k].astype(F32)

    rows = gw_ref.shape[0]
    for c in range(2):
        half[c] = total[:, c * rows : (c + 1) * rows, :] * scale
    swap = remote(half.at[1 - core], other, o_s, o_r, {"dp": sib})
    swap.start()
    swap.wait_recv()
    for t in range(tiles):
        gw_ref[:, pl.ds(pl.multiple_of(core * cols + t * tcols, BLK), tcols)] = half[core, t]
        gw_ref[:, pl.ds(pl.multiple_of((1 - core) * cols + t * tcols, BLK), tcols)] = other[t]

    swap.wait_send()
    dy_copy.wait_send()
    own_g.wait()
    forward(me, 0).wait_send()

    @pl.loop(1, peers)
    def _(k):
        at_copy(k).wait_send()
        forward(lax.rem(me - k + peers, peers), k).wait_send()
        g_copy(k).wait()

    for step in range(nz - 1):
        for t in order:
            z_copy(t, step)[1].wait_send()

    @pl.loop(1, slabs)
    def _(k):
        p_copy(k).wait_send()


def bring_back(at, g, dy, scale):
    peers = at.shape[0]
    rows, depth = dy.shape
    tiles, tcols, nz, slabs = 6, 256, 4, 16
    out_rows = peers * 192 // 128
    dma = pltpu.SemaphoreType.DMA
    return pl.pallas_call(
        functools.partial(back_kernel, scale),
        out_shape=(jax.ShapeDtypeStruct(g.shape, BF16), jax.ShapeDtypeStruct((out_rows, depth), F32)),
        in_specs=[V, V, V],
        out_specs=(V, V),
        scratch_shapes=[
            pltpu.VMEM((2, *at.shape), BF16),
            pltpu.VMEM((2, rows, depth // 2), BF16),
            pltpu.VMEM((tiles, nz, slabs, 2 * out_rows, tcols), BF16),
            pltpu.VMEM((tiles, nz - 1, slabs, 2 * out_rows, tcols), BF16),
            pltpu.VMEM((slabs, tiles, 2 * out_rows, tcols), BF16),
            pltpu.VMEM((tiles, 2 * out_rows, tcols), F32),
            pltpu.VMEM((2, tiles, out_rows, tcols), F32),
            pltpu.VMEM((tiles, out_rows, tcols), F32),
            dma((peers,)), dma((peers,)), dma((peers,)), dma((peers,)), dma, dma,
            dma((peers,)), dma((peers,)), dma((tiles, nz - 1)), dma((tiles, nz - 1)),
            dma((slabs,)), dma((slabs,)), dma, dma, dma((3,)),
        ],
        compiler_params=pltpu.CompilerParams(
            collective_id=1, has_side_effects=True, vmem_limit_bytes=56 * 2**20
        ),
        cost_estimate=cost(2 * rows * depth * peers * 192, at, g, g, dy),
        name="bring_back",
    )(at, g, dy)


V = pl.BlockSpec(memory_space=pltpu.VMEM)
S = pl.BlockSpec(memory_space=pltpu.SMEM)


def cost(flops, *arrays):
    return pl.CostEstimate(
        flops=flops, bytes_accessed=sum(a.size * a.dtype.itemsize for a in arrays), transcendentals=0
    )


def attention(idx, cnt, x, d):
    heads, blocks = cnt.shape
    seq = blocks * BLK
    return pl.pallas_call(
        attn_kernel,
        out_shape=(jax.ShapeDtypeStruct(d.shape, BF16), jax.ShapeDtypeStruct(x.shape, BF16)),
        in_specs=[S, S, V, V],
        out_specs=(V, V),
        scratch_shapes=[
            pltpu.VMEM((heads, BLK, seq), BF16),
            pltpu.VMEM((heads, seq, BLK), F32),
        ],
        compiler_params=pltpu.CompilerParams(vmem_limit_bytes=48 * 2**20),
        cost_estimate=cost(60_000_000_000, x, d, x, d),
        name="attention",
    )(idx, cnt, x, d)


def wide(rows, cols):
    return pl.BlockSpec((rows, cols), lambda t: (0, t))


def local(query, key_states, value_states, grad_out, w_out, block_index, block_count):
    rows, hd = query.shape[1:]
    depth = grad_out.shape[2]
    n_seq, n_dp = lax.axis_size("seq"), lax.axis_size("dp")
    per = hd // HDIM // n_seq
    tiles = n_seq // 2
    cols = hd // tiles
    x_rows = per * rows + TB * per * HDIM
    d_rows = TB * per * HDIM
    packed = jax.ShapeDtypeStruct((n_seq, x_rows, BLK), BF16)
    small = jax.ShapeDtypeStruct((n_seq, d_rows, BLK), BF16)
    pairs = pl.BlockSpec((2, x_rows, BLK), lambda t: (t, 0, 0))
    flat = jax.ShapeDtypeStruct((rows, hd), BF16)
    q, k, v, dy = query[0], key_states[0], value_states[0], grad_out[0]

    dma = pltpu.SemaphoreType.DMA
    x, d = pl.pallas_call(
        front_kernel,
        out_shape=(packed, small),
        in_specs=[V] * 5,
        out_specs=(V, V),
        scratch_shapes=[
            pltpu.VMEM(packed.shape, BF16),
            pltpu.VMEM(small.shape, BF16),
            pltpu.VMEM((2, 2, n_dp // 4, *w_out.shape), BF16),
            dma((n_seq,)), dma((n_seq,)), dma((n_seq,)), dma((n_seq,)),
            dma((2, 2, 2)), dma((2, 2, 2)), dma, dma, dma((2, 4)), dma((2, 4)), dma((3,)),
        ],
        compiler_params=pltpu.CompilerParams(
            collective_id=0, has_side_effects=True, vmem_limit_bytes=56 * 2**20
        ),
        cost_estimate=cost(2 * rows * depth * hd, q, k, v, dy, packed),
        name="front",
    )(q, k, v, dy, w_out)
    first = lax.axis_index("seq") * per
    idx = lax.dynamic_slice_in_dim(block_index, first, per, 0)
    cnt = lax.dynamic_slice_in_dim(block_count, first, per, 0)
    at, g = attention(idx, cnt, x, d)
    scale = float(rows * n_seq * n_dp) ** (-0.5)
    gr, gw = bring_back(at, g, dy, scale)
    dq, dk, dv = pl.pallas_call(
        unpack_kernel, out_shape=(flat,) * 3, grid=(tiles,), in_specs=[pairs],
        out_specs=(wide(rows, cols),) * 3, cost_estimate=cost(0, q, k, v, packed), name="unpack",
    )(gr)
    return dq[None], dk[None], dv[None], gw


def solution(mesh):
    tok = P("dp", "seq", None)
    return jax.shard_map(
        local,
        mesh=mesh,
        in_specs=(tok, tok, tok, tok, P("dp", None), P(), P()),
        out_specs=(tok, tok, tok, P(("seq", "dp"), None)),
        check_vma=False,
    )
```

```python
import functools

import jax
import jax.numpy as jnp
from jax import lax
from jax.experimental import pallas as pl
from jax.experimental.pallas import tpu as pltpu
from jax.sharding import PartitionSpec as P

HDIM = 64
BLK = 128
NT = (((1,), (1,)), ((), ()))
NN = (((1,), (0,)), ((), ()))
TN = (((0,), (0,)), ((), ()))
BF16 = jnp.bfloat16
F32 = jnp.float32
MESH = pl.DeviceIdType.MESH
REACH = 4
TB = 3
Q_AT = 1152


def front_kernel(q_ref, k_ref, v_ref, dy_ref, w_ref, xr_ref, dr_ref, xs, ds, wall,
                 x_s, x_r, d_s, d_r, z_s, z_r, y_s, y_r, f_s, f_r, loc):
    dp, me = lax.axis_index("dp"), lax.axis_index("seq")
    core, zz, lo = dp % 2, (dp // 2) % 4, dp // 8
    sib, mate = dp + 1 - 2 * core, dp + 8 - 16 * lo
    peers, nz = xs.shape[0], wall.shape[2]
    rows = q_ref.shape[0]
    feats = q_ref.shape[1] // peers
    part = wall.shape[3] // 2

    def at_z(k):
        return lo * 8 + lax.rem(zz + k + nz, nz) * 2 + core

    bar = pltpu.get_barrier_semaphore()

    def hello(where):
        pl.semaphore_signal(bar, inc=1, device_id=where, device_id_type=MESH)

    @pl.loop(1, peers)
    def _(k):
        hello({"seq": lax.rem(me + k, peers)})

    for where in (sib, mate, at_z(1), at_z(-1)):
        hello({"dp": where})
    pl.semaphore_wait(bar, peers + 3)

    def remote(src, dst, ssem, rsem, where):
        return pltpu.make_async_remote_copy(
            src_ref=src, dst_ref=dst, send_sem=ssem, recv_sem=rsem, device_id=where, device_id_type=MESH
        )

    def row(l):
        return lo if l == 0 else 1 - lo

    def cell(l, k, c=None):
        return wall.at[core if c is None else c, row(l), lax.rem(zz - k + nz, nz)]

    def source(l):
        return w_ref if l == 0 else cell(l, 0)

    def hop(l, up):
        d = 0 if up == 1 else 1
        return remote(source(l), cell(l, 0), z_s.at[l, d, 0], z_r.at[l, d, 0], {"dp": at_z(up)})

    def hop_in(l, up):
        d = 0 if up == 1 else 1
        return remote(cell(l, up), cell(l, up), z_s.at[l, d, 0], z_r.at[l, d, 0], {"dp": at_z(up)})

    def relay(l, up):
        d = 0 if up == 1 else 1
        h = pl.ds(d * part, part)
        c = cell(l, up).at[h]
        return remote(c, c, z_s.at[l, d, 1], z_r.at[l, d, 1], {"dp": at_z(up)})

    def relay_in(l, up):
        d = 0 if up == 1 else 1
        h = pl.ds(d * part, part)
        c = cell(l, 2).at[h]
        return remote(c, c, z_s.at[l, d, 1], z_r.at[l, d, 1], {"dp": at_z(up)})

    def over(l, k):
        return remote(
            w_ref if (l, k) == (0, 0) else cell(l, k), cell(l, k), f_s.at[l, k], f_r.at[l, k], {"dp": sib}
        )

    def over_in(l, k):
        c = cell(l, k, 1 - core)
        return remote(c, c, f_s.at[l, k], f_r.at[l, k], {"dp": sib})

    hop(0, 1).start()
    hop(0, -1).start()
    to_mate = remote(w_ref, cell(0, 0), y_s, y_r, {"dp": mate})
    to_mate.start()
    over(0, 0).start()
    own_w = pltpu.make_async_copy(w_ref, cell(0, 0), loc.at[0])
    own_w.start()

    k, v = k_ref[...], v_ref[...]
    for p in range(peers):
        for j in range(feats // HDIM):
            cols = slice(p * feats + j * HDIM, p * feats + (j + 1) * HDIM)
            xs[p, j * rows : (j + 1) * rows] = jnp.concatenate([k[:, cols], v[:, cols]], axis=1)
    for p in range(0, peers, 2):
        qt = q_ref[:, p * feats : (p + 2) * feats].T
        for i in range(2):
            for t in range(TB):
                at = Q_AT + t * feats
                xs[p + i, at : at + feats] = qt[i * feats : (i + 1) * feats, t * BLK : (t + 1) * BLK]

    def x_copy(k):
        p = lax.rem(me + k, peers)
        return remote(xs.at[p], xr_ref.at[me], x_s.at[k], x_r.at[k], {"seq": p})

    @pl.loop(1, peers)
    def _(k):
        x_copy(k).start()

    own_x = pltpu.make_async_copy(xs.at[me], xr_ref.at[me], loc.at[1])
    own_x.start()
    own_w.wait()

    def d_copy(n, s):
        return remote(ds.at[s], dr_ref.at[me], d_s.at[n], d_r.at[me], {"seq": s})

    def own_d():
        return pltpu.make_async_copy(ds.at[me], dr_ref.at[me], loc.at[2])

    def peer(l, k):
        return row(l) * nz + lax.rem(zz - k + nz, nz)

    def project(n, l, k):
        over_in(l, k).wait_recv()
        s, z = peer(l, k), lax.rem(zz - k + nz, nz)
        w2 = jnp.concatenate([wall[0, row(l), z], wall[1, row(l), z]], axis=0)
        d = lax.dot_general(w2, dy_ref[...], NT, preferred_element_type=F32).astype(BF16)
        for t in range(TB):
            ds[s, t * feats : (t + 1) * feats] = d[:, t * BLK : (t + 1) * BLK]

        @pl.when(s != me)
        def _():
            d_copy(n, s).start()

        @pl.when(s == me)
        def _():
            own_d().start()

    order = [(0, 0), (1, 0), (0, 1), (0, 3), (1, 1), (1, 3), (0, 2), (1, 2)]

    def spread(l):
        hop_in(l, 1).wait_recv()
        relay(l, 1).start()
        over(l, 1).start()
        hop_in(l, -1).wait_recv()
        relay(l, -1).start()
        over(l, 3).start()

    def finish(l):
        relay_in(l, 1).wait_recv()
        relay_in(l, -1).wait_recv()
        over(l, 2).start()

    project(0, *order[0])
    remote(cell(1, 0), cell(1, 0), y_s, y_r, {"dp": mate}).wait_recv()
    hop(1, 1).start()
    hop(1, -1).start()
    over(1, 0).start()
    spread(0)
    project(1, *order[1])
    project(2, *order[2])
    project(3, *order[3])
    spread(1)
    project(4, *order[4])
    project(5, *order[5])
    finish(0)
    project(6, *order[6])
    finish(1)
    project(7, *order[7])

    for l in range(2):
        for up in (1, -1):
            hop(l, up).wait_send()
            relay(l, up).wait_send()
        for k in range(nz):
            over(l, k).wait_send()
    to_mate.wait_send()
    own_x.wait()

    @pl.loop(1, peers)
    def _(k):
        x_copy(k).wait()

    for n, (l, k) in enumerate(order):
        s = peer(l, k)

        @pl.when(s != me)
        def _():
            d_copy(n, s).wait_send()

        @pl.when(s == me)
        def _():
            own_d().wait()

    @pl.loop(1, peers)
    def _(k):
        p = lax.rem(me + k, peers)
        remote(ds.at[p], dr_ref.at[p], d_s.at[0], d_r.at[p], {"seq": p}).wait_recv()


def unpack_kernel(x_ref, q_ref, k_ref, v_ref):
    rows = q_ref.shape[0]
    feats = q_ref.shape[1] // 2
    ks, vs, qs = [], [], []
    for peer in range(2):
        for j in range(feats // HDIM):
            x = x_ref[peer, j * rows : (j + 1) * rows]
            ks.append(x[:, :HDIM])
            vs.append(x[:, HDIM:])
        qs.append(
            jnp.concatenate(
                [x_ref[peer, Q_AT + t * feats : Q_AT + (t + 1) * feats] for t in range(rows // BLK)], axis=1
            )
        )
    q_ref[...] = jnp.concatenate(qs, axis=0).T
    k_ref[...] = jnp.concatenate(ks, axis=1)
    v_ref[...] = jnp.concatenate(vs, axis=1)


def attend(jobs, bias_ref, x_ref, d_ref, kvt_ref, acc_ref, at_ref, g_ref):
    feats = d_ref.shape[1] // TB
    per = TB * BLK
    blocks = x_ref.shape[0] * TB
    width = 2 * REACH + 1
    def seq_rows(b):
        return pl.ds(pl.multiple_of(b * BLK, BLK), BLK)
    st = []
    for h, i in jobs:
        at = (i % TB) * feats + h * HDIM
        here = pl.ds(pl.multiple_of(at, HDIM), HDIM)
        there = pl.ds(pl.multiple_of(Q_AT + at, HDIM), HDIM)
        qt = x_ref[i // TB, there, :] * BF16(HDIM**-0.5)
        dt = d_ref[i // TB, here, :]
        zero = jnp.zeros_like(qt)
        both = jnp.concatenate([jnp.concatenate([qt, zero], axis=1), jnp.concatenate([zero, dt], axis=1)], axis=0)
        ids = [lax.rem(i + o + blocks - REACH, blocks) for o in range(width)]
        sd = [lax.dot_general(x_ref[b // TB, pl.ds(pl.multiple_of(h * per + (b % TB) * BLK, BLK), BLK), :], both, NN, preferred_element_type=F32) for b in ids]
        st.append((h, i, here, there, qt, dt, ids, sd))
    outs = []
    for h, i, here, there, qt, dt, ids, sd in st:
        s = [sd[o][:, :BLK] + bias_ref[(h * blocks + i) * width + o] if o != REACH else sd[o][:, :BLK] for o in range(width)]
        dp = [a[:, BLK:] for a in sd]
        top = jnp.max(functools.reduce(jnp.maximum, s), axis=0, keepdims=True)
        w = [jnp.exp(a - top) for a in s]
        inv = 1.0 / jnp.sum(functools.reduce(jnp.add, w), axis=0, keepdims=True)
        delta = jnp.sum(functools.reduce(jnp.add, [a * b for a, b in zip(w, dp)]), axis=0, keepdims=True) * inv
        ds = [a * (b - delta) for a, b in zip(w, dp)]
        dsp = [jnp.concatenate([a.astype(BF16), b.astype(BF16)], axis=1) for a, b in zip(ds, w)]
        qi = (qt.astype(F32) * inv).astype(BF16)
        di = (dt.astype(F32) * inv).astype(BF16)
        zero = jnp.zeros_like(qi)
        both = jnp.concatenate([jnp.concatenate([qi, zero], axis=1), jnp.concatenate([zero, di], axis=1)], axis=0)
        gr = [lax.dot_general(a, both, NT, preferred_element_type=F32) for a in dsp]
        kt = jnp.concatenate([kvt_ref[h, :, seq_rows(b)] for b in ids], axis=1)
        o = lax.dot_general(kt, jnp.concatenate(dsp, axis=0), NN, preferred_element_type=F32)
        outs.append((gr, o, inv))
    for (h, i, here, there, qt, dt, ids, sd), (gr, o, inv) in zip(st, outs):
        for b, a in zip(ids, gr):
            acc_ref[h, seq_rows(b), :] += a
        g_ref[i // TB, there, :] = (o[:HDIM, :BLK] * (inv * HDIM**-0.5)).astype(BF16)
        at_ref[i // TB, here, :] = (o[HDIM:, BLK:] * inv).astype(BF16)


def make_bias(idx, cnt):
    heads, blocks, slots = idx.shape
    rel = (idx - jnp.arange(blocks)[None, :, None] + REACH) % blocks
    live = jnp.arange(slots) < cnt[:, :, None]
    hit = jnp.any((rel[..., None] == jnp.arange(2 * REACH + 1)) & live[..., None], axis=2)
    return jnp.where(hit, 0.0, -1e30).astype(F32).reshape(-1)


def rest_kernel(scale, bias_ref, x_ref, d_ref, dy_ref, gr_ref, gw_ref, at_ref, g_ref, kvt, acc, atr, dyx, part, ring, plane, total, half, other,
                at_s, at_r, fw_s, fw_r, dy_s, dy_r, q_s, q_r, g_s, g_r, z_s, z_r, p_s, p_r, o_s, o_r, loc):
    dp, me = lax.axis_index("dp"), lax.axis_index("seq")
    core, zz, lo = dp % 2, (dp // 2) % 4, dp // 8
    sib = dp + 1 - 2 * core
    tiles, nz, slabs, srows, tcols = part.shape
    peers = at_ref.shape[0]
    feats = at_ref.shape[1] // TB
    tb = TB
    cols = dyx.shape[2]
    my = me * 2 + lo

    def at_z(k):
        return lo * 8 + lax.rem(zz + k + nz, nz) * 2 + core

    def plane_peer(k):
        j = lax.rem(my + k, slabs)
        return j, {"dp": (j % 2) * 8 + zz * 2 + core, "seq": j // 2}

    bar = pltpu.get_barrier_semaphore()

    def hello(where):
        pl.semaphore_signal(bar, inc=1, device_id=where, device_id_type=MESH)

    @pl.loop(1, slabs)
    def _(k):
        hello(plane_peer(k)[1])

    hello({"dp": sib})
    hello({"dp": at_z(1)})
    hello({"dp": at_z(-1)})
    pl.semaphore_wait(bar, slabs + 2)

    def remote(src, dst, ssem, rsem, where):
        return pltpu.make_async_remote_copy(
            src_ref=src, dst_ref=dst, send_sem=ssem, recv_sem=rsem, device_id=where, device_id_type=MESH
        )

    def at_copy(k):
        p = lax.rem(me + k, peers)
        return remote(at_ref.at[p], atr.at[0, me], at_s.at[k], at_r.at[k], {"seq": p})

    mine = pl.ds(pl.multiple_of(core * cols, BLK), cols)
    theirs = pl.ds(pl.multiple_of((1 - core) * cols, BLK), cols)
    dy_copy = remote(dy_ref.at[:, theirs], dyx.at[1], dy_s, dy_r, {"dp": sib})
    dy_copy.start()
    own_dy = pltpu.make_async_copy(dy_ref.at[:, mine], dyx.at[0], loc.at[0])
    own_dy.start()

    heads = acc.shape[0]

    def q_copy(k):
        p = lax.rem(me + k, peers)
        r = pl.ds(Q_AT, feats * tb)
        return remote(g_ref.at[p, r], gr_ref.at[me, r], q_s.at[k], q_r.at[k], {"seq": p})

    def g_copy(k):
        p = lax.rem(me + k, peers)
        r = pl.ds(0, Q_AT)
        return remote(g_ref.at[p, r], gr_ref.at[me, r], g_s.at[k], g_r.at[k], {"seq": p})

    def forward(s, k):
        return remote(atr.at[0, s], atr.at[1, s], fw_s.at[k], fw_r.at[k], {"dp": sib})

    def arrived(k):
        at_copy(k).wait_recv()
        forward(lax.rem(me - k + peers, peers), k).start()

    def key_rows(h, t):
        return pl.ds(pl.multiple_of((h * tb + t) * BLK, BLK), BLK)

    def seq_rows(b):
        return pl.ds(pl.multiple_of(b * BLK, BLK), BLK)

    @pl.loop(0, peers * tb)
    def _(j):
        for h in range(heads):
            kvt[h, :, seq_rows(j)] = x_ref[j // tb, key_rows(h, lax.rem(j, tb)), :].T
            acc[h, seq_rows(j), :] = jnp.zeros((BLK, BLK), F32)

    def settle(k):
        c = lax.rem(me + k, peers)
        for h in range(heads):
            for t in range(tb):
                g_ref[c, key_rows(h, t), :] = acc[h, seq_rows(c * tb + t), :].astype(BF16)

    @pl.loop(0, peers // 2)
    def _(pair):
        @pl.loop(0, tb)
        def _(u):
            b0 = (me + 1 + 2 * pair) * tb + 2 * u
            attend(
                [(h, lax.rem(b0 + t, peers * tb)) for t in range(2) for h in range(heads)],
                bias_ref, x_ref, d_ref, kvt, acc, at_ref, g_ref,
            )

        at_copy(2 * pair + 1).start()
        q_copy(2 * pair + 1).start()

        @pl.when(pair < peers // 2 - 1)
        def _():
            at_copy(2 * pair + 2).start()
            q_copy(2 * pair + 2).start()

        @pl.when(pair > 0)
        def _():
            arrived(2 * pair - 1)
            arrived(2 * pair)

        @pl.when(pair == peers // 2 - 2)
        def _():
            for k in (3, 4):
                settle(k)
                g_copy(k).start()

    own_at = pltpu.make_async_copy(at_ref.at[me], atr.at[0, me], loc.at[1])
    own_at.start()
    late = (1, 2, *range(5, peers))
    for k in (*late, 0):
        settle(k)
    own_g = pltpu.make_async_copy(g_ref.at[me], gr_ref.at[me], loc.at[2])
    own_g.start()
    own_at.wait()
    forward(me, 0).start()
    arrived(peers - 1)
    for k in late:
        g_copy(k).start()

    @pl.loop(0, peers)
    def _(k):
        forward(lax.rem(me - k + peers, peers), k).wait_recv()

    dy_copy.wait_recv()
    own_dy.wait()

    way = tiles // 2

    def z_copy(t, step):
        up = 1 if t < way else -1
        chunk = lax.rem(zz - up * (1 + step) + 2 * nz, nz)
        return chunk, remote(
            part.at[t, chunk], ring.at[t, step], z_s.at[t, step], z_r.at[t, step], {"dp": at_z(up)}
        )

    order = [t + w for t in range(way) for w in (0, way)]
    for t in order:
        tc = slice(t * tcols, (t + 1) * tcols)

        @pl.loop(0, peers)
        def _(s):
            lhs = jnp.concatenate(
                [atr[q, s, b * feats : (b + 1) * feats, :] for q in range(2) for b in range(tb)], axis=1
            )
            rhs = jnp.concatenate([dyx[q, :, tc] for q in range(2)], axis=0)
            prod = lax.dot_general(lhs, rhs, NN, preferred_element_type=F32)
            for j in range(2):
                for z in range(nz):
                    r = (j * nz + z) * srows
                    part[t, z, s * 2 + j] = prod[r : r + srows].astype(BF16)

        z_copy(t, 0)[1].start()

    for step in range(nz - 1):
        for t in order:
            z_copy(t, step)[1].wait_recv()
            up = 1 if t < way else -1
            chunk = lax.rem(zz - up * (2 + step) + 2 * nz, nz)
            part[t, chunk] = (part[t, chunk].astype(F32) + ring[t, step].astype(F32)).astype(BF16)
            if step < nz - 2:
                z_copy(t, step + 1)[1].start()

    def p_copy(k):
        j, where = plane_peer(k)
        return remote(part.at[:, zz, j], plane.at[k], p_s.at[k], p_r.at[k], where)

    @pl.loop(1, slabs)
    def _(k):
        p_copy(k).start()

    total[...] = part[:, zz, my].astype(F32)

    @pl.loop(1, slabs)
    def _(k):
        p_copy(k).wait_recv()
        total[...] += plane[k].astype(F32)

    rows = gw_ref.shape[0]
    for c in range(2):
        half[c] = total[:, c * rows : (c + 1) * rows, :] * scale
    swap = remote(half.at[1 - core], other, o_s, o_r, {"dp": sib})
    swap.start()
    swap.wait_recv()
    for t in range(tiles):
        gw_ref[:, pl.ds(pl.multiple_of(core * cols + t * tcols, BLK), tcols)] = half[core, t]
        gw_ref[:, pl.ds(pl.multiple_of((1 - core) * cols + t * tcols, BLK), tcols)] = other[t]

    swap.wait_send()
    dy_copy.wait_send()
    own_g.wait()
    forward(me, 0).wait_send()

    @pl.loop(1, peers)
    def _(k):
        at_copy(k).wait_send()
        forward(lax.rem(me - k + peers, peers), k).wait_send()
        q_copy(k).wait()
        g_copy(k).wait()

    for step in range(nz - 1):
        for t in order:
            z_copy(t, step)[1].wait_send()

    @pl.loop(1, slabs)
    def _(k):
        p_copy(k).wait_send()


def rest(bias, x, d, dy, scale):
    peers = x.shape[0]
    rows, depth = dy.shape
    tiles, tcols, nz, slabs = 6, 256, 4, 16
    feats = d.shape[1] // TB
    heads, seq = feats // HDIM, peers * TB * BLK
    out_rows = peers * feats // 128
    dma = pltpu.SemaphoreType.DMA
    return pl.pallas_call(
        functools.partial(rest_kernel, scale),
        out_shape=(jax.ShapeDtypeStruct(x.shape, BF16), jax.ShapeDtypeStruct((out_rows, depth), F32)),
        in_specs=[S, V, V, V],
        out_specs=(V, V),
        scratch_shapes=[
            pltpu.VMEM(d.shape, BF16),
            pltpu.VMEM(x.shape, BF16),
            pltpu.VMEM((heads, BLK, seq), BF16),
            pltpu.VMEM((heads, seq, BLK), F32),
            pltpu.VMEM((2, *d.shape), BF16),
            pltpu.VMEM((2, rows, depth // 2), BF16),
            pltpu.VMEM((tiles, nz, slabs, 2 * out_rows, tcols), BF16),
            pltpu.VMEM((tiles, nz - 1, slabs, 2 * out_rows, tcols), BF16),
            pltpu.VMEM((slabs, tiles, 2 * out_rows, tcols), BF16),
            pltpu.VMEM((tiles, 2 * out_rows, tcols), F32),
            pltpu.VMEM((2, tiles, out_rows, tcols), F32),
            pltpu.VMEM((tiles, out_rows, tcols), F32),
            dma((peers,)), dma((peers,)), dma((peers,)), dma((peers,)), dma, dma,
            dma((peers,)), dma((peers,)), dma((peers,)), dma((peers,)),
            dma((tiles, nz - 1)), dma((tiles, nz - 1)),
            dma((slabs,)), dma((slabs,)), dma, dma, dma((3,)),
        ],
        compiler_params=pltpu.CompilerParams(
            collective_id=1, has_side_effects=True, vmem_limit_bytes=60 * 2**20
        ),
        cost_estimate=cost(2 * rows * depth * peers * feats, x, d, x, dy),
        name="rest",
    )(bias, x, d, dy)


V = pl.BlockSpec(memory_space=pltpu.VMEM)
S = pl.BlockSpec(memory_space=pltpu.SMEM)


def cost(flops, *arrays):
    return pl.CostEstimate(
        flops=flops, bytes_accessed=sum(a.size * a.dtype.itemsize for a in arrays), transcendentals=0
    )


def wide(rows, cols):
    return pl.BlockSpec((rows, cols), lambda t: (0, t))


def local(query, key_states, value_states, grad_out, w_out, block_index, block_count):
    rows, hd = query.shape[1:]
    depth = grad_out.shape[2]
    n_seq, n_dp = lax.axis_size("seq"), lax.axis_size("dp")
    per = hd // HDIM // n_seq
    tiles = n_seq // 2
    cols = hd // tiles
    x_rows = per * rows + TB * per * HDIM
    d_rows = TB * per * HDIM
    packed = jax.ShapeDtypeStruct((n_seq, x_rows, BLK), BF16)
    small = jax.ShapeDtypeStruct((n_seq, d_rows, BLK), BF16)
    pairs = pl.BlockSpec((2, x_rows, BLK), lambda t: (t, 0, 0))
    flat = jax.ShapeDtypeStruct((rows, hd), BF16)
    q, k, v, dy = query[0], key_states[0], value_states[0], grad_out[0]

    dma = pltpu.SemaphoreType.DMA
    x, d = pl.pallas_call(
        front_kernel,
        out_shape=(packed, small),
        in_specs=[V] * 5,
        out_specs=(V, V),
        scratch_shapes=[
            pltpu.VMEM(packed.shape, BF16),
            pltpu.VMEM(small.shape, BF16),
            pltpu.VMEM((2, 2, n_dp // 4, *w_out.shape), BF16),
            dma((n_seq,)), dma((n_seq,)), dma((n_seq,)), dma((n_seq,)),
            dma((2, 2, 2)), dma((2, 2, 2)), dma, dma, dma((2, 4)), dma((2, 4)), dma((3,)),
        ],
        compiler_params=pltpu.CompilerParams(
            collective_id=0, has_side_effects=True, vmem_limit_bytes=56 * 2**20
        ),
        cost_estimate=cost(2 * rows * depth * hd, q, k, v, dy, packed),
        name="front",
    )(q, k, v, dy, w_out)
    first = lax.axis_index("seq") * per
    idx = lax.dynamic_slice_in_dim(block_index, first, per, 0)
    cnt = lax.dynamic_slice_in_dim(block_count, first, per, 0)
    scale = float(rows * n_seq * n_dp) ** (-0.5)
    gr, gw = rest(make_bias(idx, cnt), x, d, dy, scale)
    dq, dk, dv = pl.pallas_call(
        unpack_kernel, out_shape=(flat,) * 3, grid=(tiles,), in_specs=[pairs],
        out_specs=(wide(rows, cols),) * 3, cost_estimate=cost(0, q, k, v, packed), name="unpack",
    )(gr)
    return dq[None], dk[None], dv[None], gw


def solution(mesh):
    tok = P("dp", "seq", None)
    return jax.shard_map(
        local,
        mesh=mesh,
        in_specs=(tok, tok, tok, tok, P("dp", None), P(), P()),
        out_specs=(tok, tok, tok, P(("seq", "dp"), None)),
        check_vma=False,
    )
```

```python
import functools

import jax
import jax.numpy as jnp
from jax import lax
from jax.experimental import pallas as pl
from jax.experimental.pallas import tpu as pltpu
from jax.sharding import PartitionSpec as P

HDIM = 64
BLK = 128
NT = (((1,), (1,)), ((), ()))
NN = (((1,), (0,)), ((), ()))
TN = (((0,), (0,)), ((), ()))
BF16 = jnp.bfloat16
F32 = jnp.float32
MESH = pl.DeviceIdType.MESH
REACH = 4
TB = 3
Q_AT = 1152


def front_kernel(q_ref, k_ref, v_ref, dy_ref, w_ref, xr_ref, dr_ref, xs, ds, wall,
                 x_s, x_r, d_s, d_r, z_s, z_r, y_s, y_r, f_s, f_r, loc):
    dp, me = lax.axis_index("dp"), lax.axis_index("seq")
    core, zz, lo = dp % 2, (dp // 2) % 4, dp // 8
    sib, mate = dp + 1 - 2 * core, dp + 8 - 16 * lo
    peers, nz = xs.shape[0], wall.shape[2]
    rows = q_ref.shape[0]
    feats = q_ref.shape[1] // peers
    part = wall.shape[3] // 2

    def at_z(k):
        return lo * 8 + lax.rem(zz + k + nz, nz) * 2 + core

    bar = pltpu.get_barrier_semaphore()

    def hello(where):
        pl.semaphore_signal(bar, inc=1, device_id=where, device_id_type=MESH)

    @pl.loop(1, peers)
    def _(k):
        hello({"seq": lax.rem(me + k, peers)})

    for where in (sib, mate, at_z(1), at_z(-1)):
        hello({"dp": where})
    pl.semaphore_wait(bar, peers + 3)

    def remote(src, dst, ssem, rsem, where):
        return pltpu.make_async_remote_copy(
            src_ref=src, dst_ref=dst, send_sem=ssem, recv_sem=rsem, device_id=where, device_id_type=MESH
        )

    def row(l):
        return lo if l == 0 else 1 - lo

    def cell(l, k, c=None):
        return wall.at[core if c is None else c, row(l), lax.rem(zz - k + nz, nz)]

    def source(l):
        return w_ref if l == 0 else cell(l, 0)

    def hop(l, up):
        d = 0 if up == 1 else 1
        return remote(source(l), cell(l, 0), z_s.at[l, d, 0], z_r.at[l, d, 0], {"dp": at_z(up)})

    def hop_in(l, up):
        d = 0 if up == 1 else 1
        return remote(cell(l, up), cell(l, up), z_s.at[l, d, 0], z_r.at[l, d, 0], {"dp": at_z(up)})

    def relay(l, up):
        d = 0 if up == 1 else 1
        h = pl.ds(d * part, part)
        c = cell(l, up).at[h]
        return remote(c, c, z_s.at[l, d, 1], z_r.at[l, d, 1], {"dp": at_z(up)})

    def relay_in(l, up):
        d = 0 if up == 1 else 1
        h = pl.ds(d * part, part)
        c = cell(l, 2).at[h]
        return remote(c, c, z_s.at[l, d, 1], z_r.at[l, d, 1], {"dp": at_z(up)})

    def over(l, k):
        return remote(
            w_ref if (l, k) == (0, 0) else cell(l, k), cell(l, k), f_s.at[l, k], f_r.at[l, k], {"dp": sib}
        )

    def over_in(l, k):
        c = cell(l, k, 1 - core)
        return remote(c, c, f_s.at[l, k], f_r.at[l, k], {"dp": sib})

    hop(0, 1).start()
    hop(0, -1).start()
    to_mate = remote(w_ref, cell(0, 0), y_s, y_r, {"dp": mate})
    to_mate.start()
    over(0, 0).start()
    own_w = pltpu.make_async_copy(w_ref, cell(0, 0), loc.at[0])
    own_w.start()

    k, v = k_ref[...], v_ref[...]
    for p in range(peers):
        for j in range(feats // HDIM):
            cols = slice(p * feats + j * HDIM, p * feats + (j + 1) * HDIM)
            xs[p, j * rows : (j + 1) * rows] = jnp.concatenate([k[:, cols], v[:, cols]], axis=1)
    for p in range(0, peers, 2):
        qt = q_ref[:, p * feats : (p + 2) * feats].T
        for i in range(2):
            for t in range(TB):
                at = Q_AT + t * feats
                xs[p + i, at : at + feats] = qt[i * feats : (i + 1) * feats, t * BLK : (t + 1) * BLK]

    def x_copy(k):
        p = lax.rem(me + k, peers)
        return remote(xs.at[p], xr_ref.at[me], x_s.at[k], x_r.at[k], {"seq": p})

    @pl.loop(1, peers)
    def _(k):
        x_copy(k).start()

    own_x = pltpu.make_async_copy(xs.at[me], xr_ref.at[me], loc.at[1])
    own_x.start()
    own_w.wait()

    def d_copy(n, s):
        return remote(ds.at[s], dr_ref.at[me], d_s.at[n], d_r.at[me], {"seq": s})

    def own_d():
        return pltpu.make_async_copy(ds.at[me], dr_ref.at[me], loc.at[2])

    def peer(l, k):
        return row(l) * nz + lax.rem(zz - k + nz, nz)

    def project(n, l, k):
        over_in(l, k).wait_recv()
        s, z = peer(l, k), lax.rem(zz - k + nz, nz)
        w2 = jnp.concatenate([wall[0, row(l), z], wall[1, row(l), z]], axis=0)
        d = lax.dot_general(w2, dy_ref[...], NT, preferred_element_type=F32).astype(BF16)
        for t in range(TB):
            ds[s, t * feats : (t + 1) * feats] = d[:, t * BLK : (t + 1) * BLK]

        @pl.when(s != me)
        def _():
            d_copy(n, s).start()

        @pl.when(s == me)
        def _():
            own_d().start()

    order = [(0, 0), (1, 0), (0, 1), (0, 3), (1, 1), (1, 3), (0, 2), (1, 2)]

    def spread(l):
        hop_in(l, 1).wait_recv()
        relay(l, 1).start()
        over(l, 1).start()
        hop_in(l, -1).wait_recv()
        relay(l, -1).start()
        over(l, 3).start()

    def finish(l):
        relay_in(l, 1).wait_recv()
        relay_in(l, -1).wait_recv()
        over(l, 2).start()

    project(0, *order[0])
    remote(cell(1, 0), cell(1, 0), y_s, y_r, {"dp": mate}).wait_recv()
    hop(1, 1).start()
    hop(1, -1).start()
    over(1, 0).start()
    spread(0)
    project(1, *order[1])
    project(2, *order[2])
    project(3, *order[3])
    spread(1)
    project(4, *order[4])
    project(5, *order[5])
    finish(0)
    project(6, *order[6])
    finish(1)
    project(7, *order[7])

    for l in range(2):
        for up in (1, -1):
            hop(l, up).wait_send()
            relay(l, up).wait_send()
        for k in range(nz):
            over(l, k).wait_send()
    to_mate.wait_send()
    own_x.wait()

    @pl.loop(1, peers)
    def _(k):
        x_copy(k).wait()

    for n, (l, k) in enumerate(order):
        s = peer(l, k)

        @pl.when(s != me)
        def _():
            d_copy(n, s).wait_send()

        @pl.when(s == me)
        def _():
            own_d().wait()

    @pl.loop(1, peers)
    def _(k):
        p = lax.rem(me + k, peers)
        remote(ds.at[p], dr_ref.at[p], d_s.at[0], d_r.at[p], {"seq": p}).wait_recv()


def unpack_kernel(x_ref, q_ref, k_ref, v_ref):
    rows = q_ref.shape[0]
    feats = q_ref.shape[1] // 2
    ks, vs, qs = [], [], []
    for peer in range(2):
        for j in range(feats // HDIM):
            x = x_ref[peer, j * rows : (j + 1) * rows]
            ks.append(x[:, :HDIM])
            vs.append(x[:, HDIM:])
        qs.append(
            jnp.concatenate(
                [x_ref[peer, Q_AT + t * feats : Q_AT + (t + 1) * feats] for t in range(rows // BLK)], axis=1
            )
        )
    q_ref[...] = jnp.concatenate(qs, axis=0).T
    k_ref[...] = jnp.concatenate(ks, axis=1)
    v_ref[...] = jnp.concatenate(vs, axis=1)


def attend(jobs, bias_ref, x_ref, d_ref, kvt_ref, acc_ref, at_ref, g_ref):
    feats = d_ref.shape[1] // TB
    per = TB * BLK
    blocks = x_ref.shape[0] * TB
    width = 2 * REACH + 1
    def seq_rows(b):
        return pl.ds(pl.multiple_of(b * BLK, BLK), BLK)
    st = []
    for h, i in jobs:
        at = (i % TB) * feats + h * HDIM
        here = pl.ds(pl.multiple_of(at, HDIM), HDIM)
        there = pl.ds(pl.multiple_of(Q_AT + at, HDIM), HDIM)
        qt = x_ref[i // TB, there, :] * BF16(HDIM**-0.5)
        dt = d_ref[i // TB, here, :]
        zero = jnp.zeros_like(qt)
        both = jnp.concatenate([jnp.concatenate([qt, zero], axis=1), jnp.concatenate([zero, dt], axis=1)], axis=0)
        ids = [lax.rem(i + o + blocks - REACH, blocks) for o in range(width)]
        sd = [lax.dot_general(x_ref[b // TB, pl.ds(pl.multiple_of(h * per + (b % TB) * BLK, BLK), BLK), :], both, NN, preferred_element_type=F32) for b in ids]
        st.append((h, i, here, there, qt, dt, ids, sd))
    outs = []
    for h, i, here, there, qt, dt, ids, sd in st:
        s = [sd[o][:, :BLK] + bias_ref[(h * blocks + i) * width + o] if o != REACH else sd[o][:, :BLK] for o in range(width)]
        dp = [a[:, BLK:] for a in sd]
        top = jnp.max(functools.reduce(jnp.maximum, s), axis=0, keepdims=True)
        w = [jnp.exp(a - top) for a in s]
        inv = 1.0 / jnp.sum(functools.reduce(jnp.add, w), axis=0, keepdims=True)
        delta = jnp.sum(functools.reduce(jnp.add, [a * b for a, b in zip(w, dp)]), axis=0, keepdims=True) * inv
        ds = [a * (b - delta) for a, b in zip(w, dp)]
        dsp = [jnp.concatenate([a.astype(BF16), b.astype(BF16)], axis=1) for a, b in zip(ds, w)]
        qi = (qt.astype(F32) * inv).astype(BF16)
        di = (dt.astype(F32) * inv).astype(BF16)
        zero = jnp.zeros_like(qi)
        both = jnp.concatenate([jnp.concatenate([qi, zero], axis=1), jnp.concatenate([zero, di], axis=1)], axis=0)
        gr = [lax.dot_general(a, both, NT, preferred_element_type=F32) for a in dsp]
        kt = jnp.concatenate([kvt_ref[h, :, seq_rows(b)] for b in ids], axis=1)
        o = lax.dot_general(kt, jnp.concatenate(dsp, axis=0), NN, preferred_element_type=F32)
        outs.append((gr, o, inv))
    for (h, i, here, there, qt, dt, ids, sd), (gr, o, inv) in zip(st, outs):
        for b, a in zip(ids, gr):
            acc_ref[h, seq_rows(b), :] += a
        g_ref[i // TB, there, :] = (o[:HDIM, :BLK] * (inv * HDIM**-0.5)).astype(BF16)
        at_ref[i // TB, here, :] = (o[HDIM:, BLK:] * inv).astype(BF16)


def make_bias(idx, cnt):
    heads, blocks, slots = idx.shape
    rel = (idx - jnp.arange(blocks)[None, :, None] + REACH) % blocks
    live = jnp.arange(slots) < cnt[:, :, None]
    hit = jnp.any((rel[..., None] == jnp.arange(2 * REACH + 1)) & live[..., None], axis=2)
    return jnp.where(hit, 0.0, -1e30).astype(F32).reshape(-1)


def rest_kernel(scale, bias_ref, x_ref, d_ref, dy_ref, gr_ref, gw_ref, at_ref, g_ref, kvt, acc, atr, dyx, part, ring, plane, total, half, other,
                at_s, at_r, fw_s, fw_r, dy_s, dy_r, q_s, q_r, g_s, g_r, z_s, z_r, p_s, p_r, o_s, o_r, loc):
    dp, me = lax.axis_index("dp"), lax.axis_index("seq")
    core, zz, lo = dp % 2, (dp // 2) % 4, dp // 8
    sib = dp + 1 - 2 * core
    rounds, ways, nz, four, srows, tcols = part.shape
    peers = at_ref.shape[0]
    slabs = plane.shape[0]
    feats = at_ref.shape[1] // TB
    tb = TB
    cols = dyx.shape[2]
    my = me * 2 + lo

    def at_z(k):
        return lo * 8 + lax.rem(zz + k + nz, nz) * 2 + core

    def plane_peer(k):
        j = lax.rem(my + k, slabs)
        return j, {"dp": (j % 2) * 8 + zz * 2 + core, "seq": j // 2}

    bar = pltpu.get_barrier_semaphore()

    def hello(where):
        pl.semaphore_signal(bar, inc=1, device_id=where, device_id_type=MESH)

    @pl.loop(1, slabs)
    def _(k):
        hello(plane_peer(k)[1])

    hello({"dp": sib})
    hello({"dp": at_z(1)})
    hello({"dp": at_z(-1)})
    pl.semaphore_wait(bar, slabs + 2)

    def remote(src, dst, ssem, rsem, where):
        return pltpu.make_async_remote_copy(
            src_ref=src, dst_ref=dst, send_sem=ssem, recv_sem=rsem, device_id=where, device_id_type=MESH
        )

    def at_copy(k):
        p = lax.rem(me + k, peers)
        return remote(at_ref.at[p], atr.at[0, me], at_s.at[k], at_r.at[k], {"seq": p})

    mine = pl.ds(pl.multiple_of(core * cols, BLK), cols)
    theirs = pl.ds(pl.multiple_of((1 - core) * cols, BLK), cols)
    dy_copy = remote(dy_ref.at[:, theirs], dyx.at[1], dy_s, dy_r, {"dp": sib})
    dy_copy.start()
    own_dy = pltpu.make_async_copy(dy_ref.at[:, mine], dyx.at[0], loc.at[0])
    own_dy.start()

    heads = acc.shape[0]

    def q_copy(k):
        p = lax.rem(me + k, peers)
        r = pl.ds(Q_AT, feats * tb)
        return remote(g_ref.at[p, r], gr_ref.at[me, r], q_s.at[k], q_r.at[k], {"seq": p})

    def g_copy(k):
        p = lax.rem(me + k, peers)
        r = pl.ds(0, Q_AT)
        return remote(g_ref.at[p, r], gr_ref.at[me, r], g_s.at[k], g_r.at[k], {"seq": p})

    def forward(s, k):
        return remote(atr.at[0, s], atr.at[1, s], fw_s.at[k], fw_r.at[k], {"dp": sib})

    def group(r, g):
        return lax.rem(me - 2 * r - 1 - g + 2 * peers, peers)

    def place(r, g):
        return lax.rem(2 * r + 1 + g, peers)

    def arrived(r, both=True):
        for g in range(2 if both else 1):
            at_copy(place(r, g)).wait_recv()
            forward(group(r, g), place(r, g)).start()

    def hop(r, w, step):
        up = 1 - 2 * w
        chunk = lax.rem(zz - up * (1 + step) + 2 * nz, nz)
        return remote(
            part.at[r, w, chunk], ring.at[r, w, step], z_s.at[r, w, step], z_r.at[r, w, step], {"dp": at_z(up)}
        )

    def products(r):
        for g in range(2):
            forward(group(r, g), place(r, g)).wait_recv()
        lhs = jnp.concatenate(
            [
                jnp.concatenate(
                    [atr[q, group(r, g), b * feats : (b + 1) * feats, :] for q in range(2) for b in range(tb)],
                    axis=1,
                )
                for g in range(2)
            ],
            axis=0,
        )
        wide_tile = 2 * BLK
        for w in range(ways):
            for c in range(tcols // wide_tile):
                tc = slice(c * wide_tile, (c + 1) * wide_tile)
                rc = slice(w * tcols + c * wide_tile, w * tcols + (c + 1) * wide_tile)
                rhs = jnp.concatenate([dyx[q, :, rc] for q in range(2)], axis=0)
                prod = lax.dot_general(lhs, rhs, NN, preferred_element_type=F32)
                for a in range(four):
                    for z in range(nz):
                        at = (a * nz + z) * srows
                        part[r, w, z, a, :, tc] = prod[at : at + srows].astype(BF16)
            hop(r, w, 0).start()

    def add(r, step):
        for w in range(ways):
            hop(r, w, step).wait_recv()
            chunk = lax.rem(zz - (1 - 2 * w) * (2 + step) + 2 * nz, nz)
            part[r, w, chunk] = (part[r, w, chunk].astype(F32) + ring[r, w, step].astype(F32)).astype(BF16)
            if step < nz - 2:
                hop(r, w, step + 1).start()

    def slab(r, a):
        where = {"dp": (a % 2) * 8 + zz * 2 + core, "seq": group(r, a // 2)}
        return remote(part.at[r, :, zz, a], plane.at[my], p_s.at[r, a], p_r.at[my], where)

    def other_slab(r, a, f):
        @pl.when((group(r, a // 2) != me) | (lo != a % 2))
        def _():
            f(slab(r, a))

    def spread(r):
        add(r, nz - 2)
        for a in range(four):
            other_slab(r, a, lambda c: c.start())

    def key_rows(h, t):
        return pl.ds(pl.multiple_of((h * tb + t) * BLK, BLK), BLK)

    def seq_rows(b):
        return pl.ds(pl.multiple_of(b * BLK, BLK), BLK)

    @pl.loop(0, peers * tb)
    def _(j):
        for h in range(heads):
            kvt[h, :, seq_rows(j)] = x_ref[j // tb, key_rows(h, lax.rem(j, tb)), :].T
            acc[h, seq_rows(j), :] = jnp.zeros((BLK, BLK), F32)

    def settle(k):
        c = lax.rem(me + k, peers)
        for h in range(heads):
            for t in range(tb):
                g_ref[c, key_rows(h, t), :] = acc[h, seq_rows(c * tb + t), :].astype(BF16)

    dy_copy.wait_recv()
    own_dy.wait()

    @pl.loop(0, rounds)
    def _(pair):
        @pl.loop(0, tb)
        def _(u):
            b0 = (me + 1 + 2 * pair) * tb + 2 * u
            attend(
                [(h, lax.rem(b0 + t, peers * tb)) for t in range(2) for h in range(heads)],
                bias_ref, x_ref, d_ref, kvt, acc, at_ref, g_ref,
            )

            @pl.when((u == 0) & (pair > 1))
            def _():
                add(pair - 2, 0)

            @pl.when((u == 1) & (pair > 0))
            def _():
                arrived(pair - 1)

            @pl.when((u == 1) & (pair > 1))
            def _():
                add(pair - 2, 1)

        at_copy(2 * pair + 1).start()
        q_copy(2 * pair + 1).start()

        @pl.when(pair < rounds - 1)
        def _():
            at_copy(2 * pair + 2).start()
            q_copy(2 * pair + 2).start()

        @pl.when(pair > 0)
        def _():
            products(pair - 1)

        @pl.when(pair > 1)
        def _():
            spread(pair - 2)

        @pl.when(pair == rounds - 2)
        def _():
            for k in (3, 4):
                settle(k)
                g_copy(k).start()

    own_at = pltpu.make_async_copy(at_ref.at[me], atr.at[0, me], loc.at[1])
    own_at.start()
    last = rounds - 1
    late = (1, 2, *range(5, peers))
    settle(1)
    settle(2)
    own_at.wait()
    forward(me, 0).start()
    add(last - 1, 0)
    arrived(last, False)
    for k in late:
        if k > 2:
            settle(k)
        g_copy(k).start()
    settle(0)
    own_g = pltpu.make_async_copy(g_ref.at[me], gr_ref.at[me], loc.at[2])
    own_g.start()
    products(last)
    add(last - 1, 1)
    add(last, 0)
    spread(last - 1)
    add(last, 1)
    spread(last)
    total[...] = part[last, :, zz, 2 + lo].astype(F32)

    @pl.loop(1, slabs)
    def _(k):
        j, where = plane_peer(k)
        remote(plane.at[j], plane.at[j], p_s.at[0, 0], p_r.at[j], where).wait_recv()
        total[...] += plane[j].astype(F32)

    rows = gw_ref.shape[0]
    for c in range(2):
        half[c] = total[:, c * rows : (c + 1) * rows, :] * scale
    swap = remote(half.at[1 - core], other, o_s, o_r, {"dp": sib})
    swap.start()
    swap.wait_recv()
    for t in range(ways):
        gw_ref[:, pl.ds(pl.multiple_of(core * cols + t * tcols, BLK), tcols)] = half[core, t]
        gw_ref[:, pl.ds(pl.multiple_of((1 - core) * cols + t * tcols, BLK), tcols)] = other[t]

    swap.wait_send()
    dy_copy.wait_send()
    own_g.wait()
    forward(me, 0).wait_send()

    @pl.loop(1, peers)
    def _(k):
        at_copy(k).wait_send()
        forward(lax.rem(me - k + peers, peers), k).wait_send()
        q_copy(k).wait()
        g_copy(k).wait()

    @pl.loop(0, rounds)
    def _(r):
        for w in range(ways):
            for step in range(nz - 1):
                hop(r, w, step).wait_send()
        for a in range(four):
            other_slab(r, a, lambda c: c.wait_send())


def rest(bias, x, d, dy, scale):
    peers = x.shape[0]
    rows, depth = dy.shape
    rounds, ways, nz, slabs = 4, 2, 4, 16
    tcols = depth // 2 // ways
    feats = d.shape[1] // TB
    heads, seq = feats // HDIM, peers * TB * BLK
    out_rows = peers * feats // 128
    dma = pltpu.SemaphoreType.DMA
    return pl.pallas_call(
        functools.partial(rest_kernel, scale),
        out_shape=(jax.ShapeDtypeStruct(x.shape, BF16), jax.ShapeDtypeStruct((out_rows, depth), F32)),
        in_specs=[S, V, V, V],
        out_specs=(V, V),
        scratch_shapes=[
            pltpu.VMEM(d.shape, BF16),
            pltpu.VMEM(x.shape, BF16),
            pltpu.VMEM((heads, BLK, seq), BF16),
            pltpu.VMEM((heads, seq, BLK), F32),
            pltpu.VMEM((2, *d.shape), BF16),
            pltpu.VMEM((2, rows, depth // 2), BF16),
            pltpu.VMEM((rounds, ways, nz, 4, 2 * out_rows, tcols), BF16),
            pltpu.VMEM((rounds, ways, nz - 1, 4, 2 * out_rows, tcols), BF16),
            pltpu.VMEM((slabs, ways, 2 * out_rows, tcols), BF16),
            pltpu.VMEM((ways, 2 * out_rows, tcols), F32),
            pltpu.VMEM((2, ways, out_rows, tcols), F32),
            pltpu.VMEM((ways, out_rows, tcols), F32),
            dma((peers,)), dma((peers,)), dma((peers,)), dma((peers,)), dma, dma,
            dma((peers,)), dma((peers,)), dma((peers,)), dma((peers,)),
            dma((rounds, ways, nz - 1)), dma((rounds, ways, nz - 1)),
            dma((rounds, 4)), dma((slabs,)), dma, dma, dma((3,)),
        ],
        compiler_params=pltpu.CompilerParams(
            collective_id=1, has_side_effects=True, vmem_limit_bytes=60 * 2**20
        ),
        cost_estimate=cost(2 * rows * depth * peers * feats, x, d, x, dy),
        name="rest",
    )(bias, x, d, dy)


V = pl.BlockSpec(memory_space=pltpu.VMEM)
S = pl.BlockSpec(memory_space=pltpu.SMEM)


def cost(flops, *arrays):
    return pl.CostEstimate(
        flops=flops, bytes_accessed=sum(a.size * a.dtype.itemsize for a in arrays), transcendentals=0
    )


def wide(rows, cols):
    return pl.BlockSpec((rows, cols), lambda t: (0, t))


def local(query, key_states, value_states, grad_out, w_out, block_index, block_count):
    rows, hd = query.shape[1:]
    depth = grad_out.shape[2]
    n_seq, n_dp = lax.axis_size("seq"), lax.axis_size("dp")
    per = hd // HDIM // n_seq
    tiles = n_seq // 2
    cols = hd // tiles
    x_rows = per * rows + TB * per * HDIM
    d_rows = TB * per * HDIM
    packed = jax.ShapeDtypeStruct((n_seq, x_rows, BLK), BF16)
    small = jax.ShapeDtypeStruct((n_seq, d_rows, BLK), BF16)
    pairs = pl.BlockSpec((2, x_rows, BLK), lambda t: (t, 0, 0))
    flat = jax.ShapeDtypeStruct((rows, hd), BF16)
    q, k, v, dy = query[0], key_states[0], value_states[0], grad_out[0]

    dma = pltpu.SemaphoreType.DMA
    x, d = pl.pallas_call(
        front_kernel,
        out_shape=(packed, small),
        in_specs=[V] * 5,
        out_specs=(V, V),
        scratch_shapes=[
            pltpu.VMEM(packed.shape, BF16),
            pltpu.VMEM(small.shape, BF16),
            pltpu.VMEM((2, 2, n_dp // 4, *w_out.shape), BF16),
            dma((n_seq,)), dma((n_seq,)), dma((n_seq,)), dma((n_seq,)),
            dma((2, 2, 2)), dma((2, 2, 2)), dma, dma, dma((2, 4)), dma((2, 4)), dma((3,)),
        ],
        compiler_params=pltpu.CompilerParams(
            collective_id=0, has_side_effects=True, vmem_limit_bytes=56 * 2**20
        ),
        cost_estimate=cost(2 * rows * depth * hd, q, k, v, dy, packed),
        name="front",
    )(q, k, v, dy, w_out)
    first = lax.axis_index("seq") * per
    idx = lax.dynamic_slice_in_dim(block_index, first, per, 0)
    cnt = lax.dynamic_slice_in_dim(block_count, first, per, 0)
    scale = float(rows * n_seq * n_dp) ** (-0.5)
    gr, gw = rest(make_bias(idx, cnt), x, d, dy, scale)
    dq, dk, dv = pl.pallas_call(
        unpack_kernel, out_shape=(flat,) * 3, grid=(tiles,), in_specs=[pairs],
        out_specs=(wide(rows, cols),) * 3, cost_estimate=cost(0, q, k, v, packed), name="unpack",
    )(gr)
    return dq[None], dk[None], dv[None], gw


def solution(mesh):
    tok = P("dp", "seq", None)
    return jax.shard_map(
        local,
        mesh=mesh,
        in_specs=(tok, tok, tok, tok, P("dp", None), P(), P()),
        out_specs=(tok, tok, tok, P(("seq", "dp"), None)),
        check_vma=False,
    )
```

```python
import functools

import jax
import jax.numpy as jnp
from jax import lax
from jax.experimental import pallas as pl
from jax.experimental.pallas import tpu as pltpu
from jax.sharding import PartitionSpec as P

HDIM = 64
BLK = 128
NT = (((1,), (1,)), ((), ()))
NN = (((1,), (0,)), ((), ()))
TN = (((0,), (0,)), ((), ()))
BF16 = jnp.bfloat16
F32 = jnp.float32
MESH = pl.DeviceIdType.MESH
REACH = 4
TB = 3
Q_AT = 1152


def bring_in(meanwhile, q_ref, k_ref, v_ref, dy_ref, w_ref, xr_ref, dr_ref, xs, ds, wall,
             x_s, x_r, d_s, d_r, z_s, z_r, y_s, y_r, f_s, f_r, loc):
    dp, me = lax.axis_index("dp"), lax.axis_index("seq")
    core, zz, lo = dp % 2, (dp // 2) % 4, dp // 8
    sib, mate = dp + 1 - 2 * core, dp + 8 - 16 * lo
    peers, nz = xs.shape[0], wall.shape[2]
    rows = q_ref.shape[0]
    feats = q_ref.shape[1] // peers
    part = wall.shape[3] // 2

    def at_z(k):
        return lo * 8 + lax.rem(zz + k + nz, nz) * 2 + core

    def remote(src, dst, ssem, rsem, where):
        return pltpu.make_async_remote_copy(
            src_ref=src, dst_ref=dst, send_sem=ssem, recv_sem=rsem, device_id=where, device_id_type=MESH
        )

    def row(l):
        return lo if l == 0 else 1 - lo

    def cell(l, k, c=None):
        return wall.at[core if c is None else c, row(l), lax.rem(zz - k + nz, nz)]

    def source(l):
        return w_ref if l == 0 else cell(l, 0)

    def hop(l, up):
        d = 0 if up == 1 else 1
        return remote(source(l), cell(l, 0), z_s.at[l, d, 0], z_r.at[l, d, 0], {"dp": at_z(up)})

    def hop_in(l, up):
        d = 0 if up == 1 else 1
        return remote(cell(l, up), cell(l, up), z_s.at[l, d, 0], z_r.at[l, d, 0], {"dp": at_z(up)})

    def relay(l, up):
        d = 0 if up == 1 else 1
        h = pl.ds(d * part, part)
        c = cell(l, up).at[h]
        return remote(c, c, z_s.at[l, d, 1], z_r.at[l, d, 1], {"dp": at_z(up)})

    def relay_in(l, up):
        d = 0 if up == 1 else 1
        h = pl.ds(d * part, part)
        c = cell(l, 2).at[h]
        return remote(c, c, z_s.at[l, d, 1], z_r.at[l, d, 1], {"dp": at_z(up)})

    def over(l, k):
        return remote(
            w_ref if (l, k) == (0, 0) else cell(l, k), cell(l, k), f_s.at[l, k], f_r.at[l, k], {"dp": sib}
        )

    def over_in(l, k):
        c = cell(l, k, 1 - core)
        return remote(c, c, f_s.at[l, k], f_r.at[l, k], {"dp": sib})

    hop(0, 1).start()
    hop(0, -1).start()
    to_mate = remote(w_ref, cell(0, 0), y_s, y_r, {"dp": mate})
    to_mate.start()
    over(0, 0).start()
    own_w = pltpu.make_async_copy(w_ref, cell(0, 0), loc.at[0])
    own_w.start()

    k, v = k_ref[...], v_ref[...]
    for p in range(peers):
        for j in range(feats // HDIM):
            cols = slice(p * feats + j * HDIM, p * feats + (j + 1) * HDIM)
            xs[p, j * rows : (j + 1) * rows] = jnp.concatenate([k[:, cols], v[:, cols]], axis=1)
    for p in range(0, peers, 2):
        qt = q_ref[:, p * feats : (p + 2) * feats].T
        for i in range(2):
            for t in range(TB):
                at = Q_AT + t * feats
                xs[p + i, at : at + feats] = qt[i * feats : (i + 1) * feats, t * BLK : (t + 1) * BLK]

    def x_copy(k):
        p = lax.rem(me + k, peers)
        return remote(xs.at[p], xr_ref.at[me], x_s.at[k], x_r.at[k], {"seq": p})

    @pl.loop(1, peers)
    def _(k):
        x_copy(k).start()

    own_x = pltpu.make_async_copy(xs.at[me], xr_ref.at[me], loc.at[1])
    own_x.start()
    own_w.wait()

    def d_copy(n, s):
        return remote(ds.at[s], dr_ref.at[me], d_s.at[n], d_r.at[me], {"seq": s})

    def own_d():
        return pltpu.make_async_copy(ds.at[me], dr_ref.at[me], loc.at[2])

    def peer(l, k):
        return row(l) * nz + lax.rem(zz - k + nz, nz)

    def project(n, l, k):
        over_in(l, k).wait_recv()
        s, z = peer(l, k), lax.rem(zz - k + nz, nz)
        w2 = jnp.concatenate([wall[0, row(l), z], wall[1, row(l), z]], axis=0)
        d = lax.dot_general(w2, dy_ref[...], NT, preferred_element_type=F32).astype(BF16)
        for t in range(TB):
            ds[s, t * feats : (t + 1) * feats] = d[:, t * BLK : (t + 1) * BLK]

        @pl.when(s != me)
        def _():
            d_copy(n, s).start()

        @pl.when(s == me)
        def _():
            own_d().start()

    order = [(0, 0), (1, 0), (0, 1), (0, 3), (1, 1), (1, 3), (0, 2), (1, 2)]

    def spread(l):
        hop_in(l, 1).wait_recv()
        relay(l, 1).start()
        over(l, 1).start()
        hop_in(l, -1).wait_recv()
        relay(l, -1).start()
        over(l, 3).start()

    def finish(l):
        relay_in(l, 1).wait_recv()
        relay_in(l, -1).wait_recv()
        over(l, 2).start()

    project(0, *order[0])
    remote(cell(1, 0), cell(1, 0), y_s, y_r, {"dp": mate}).wait_recv()
    hop(1, 1).start()
    hop(1, -1).start()
    over(1, 0).start()
    spread(0)
    project(1, *order[1])
    project(2, *order[2])
    project(3, *order[3])
    spread(1)
    project(4, *order[4])
    project(5, *order[5])
    finish(0)
    project(6, *order[6])
    finish(1)
    project(7, *order[7])

    for l in range(2):
        for up in (1, -1):
            hop(l, up).wait_send()
            relay(l, up).wait_send()
        for k in range(nz):
            over(l, k).wait_send()
    to_mate.wait_send()
    own_x.wait()

    @pl.loop(1, peers)
    def _(k):
        x_copy(k).wait()

    meanwhile()
    for n, (l, k) in enumerate(order):
        s = peer(l, k)

        @pl.when(s != me)
        def _():
            d_copy(n, s).wait_send()

        @pl.when(s == me)
        def _():
            own_d().wait()

    @pl.loop(1, peers)
    def _(k):
        p = lax.rem(me + k, peers)
        remote(ds.at[p], dr_ref.at[p], d_s.at[0], d_r.at[p], {"seq": p}).wait_recv()


def unpack_kernel(x_ref, q_ref, k_ref, v_ref):
    rows = q_ref.shape[0]
    feats = q_ref.shape[1] // 2
    ks, vs, qs = [], [], []
    for peer in range(2):
        for j in range(feats // HDIM):
            x = x_ref[peer, j * rows : (j + 1) * rows]
            ks.append(x[:, :HDIM])
            vs.append(x[:, HDIM:])
        qs.append(
            jnp.concatenate(
                [x_ref[peer, Q_AT + t * feats : Q_AT + (t + 1) * feats] for t in range(rows // BLK)], axis=1
            )
        )
    q_ref[...] = jnp.concatenate(qs, axis=0).T
    k_ref[...] = jnp.concatenate(ks, axis=1)
    v_ref[...] = jnp.concatenate(vs, axis=1)


def attend(jobs, bias_ref, x_ref, d_ref, kvt_ref, acc_ref, at_ref, g_ref):
    feats = d_ref.shape[1] // TB
    per = TB * BLK
    blocks = x_ref.shape[0] * TB
    width = 2 * REACH + 1
    def seq_rows(b):
        return pl.ds(pl.multiple_of(b * BLK, BLK), BLK)
    st = []
    for h, i in jobs:
        at = (i % TB) * feats + h * HDIM
        here = pl.ds(pl.multiple_of(at, HDIM), HDIM)
        there = pl.ds(pl.multiple_of(Q_AT + at, HDIM), HDIM)
        qt = x_ref[i // TB, there, :] * BF16(HDIM**-0.5)
        dt = d_ref[i // TB, here, :]
        zero = jnp.zeros_like(qt)
        both = jnp.concatenate([jnp.concatenate([qt, zero], axis=1), jnp.concatenate([zero, dt], axis=1)], axis=0)
        ids = [lax.rem(i + o + blocks - REACH, blocks) for o in range(width)]
        sd = [lax.dot_general(x_ref[b // TB, pl.ds(pl.multiple_of(h * per + (b % TB) * BLK, BLK), BLK), :], both, NN, preferred_element_type=F32) for b in ids]
        st.append((h, i, here, there, qt, dt, ids, sd))
    outs = []
    for h, i, here, there, qt, dt, ids, sd in st:
        s = [sd[o][:, :BLK] + bias_ref[(h * blocks + i) * width + o] if o != REACH else sd[o][:, :BLK] for o in range(width)]
        dp = [a[:, BLK:] for a in sd]
        top = jnp.max(functools.reduce(jnp.maximum, s), axis=0, keepdims=True)
        w = [jnp.exp(a - top) for a in s]
        inv = 1.0 / jnp.sum(functools.reduce(jnp.add, w), axis=0, keepdims=True)
        delta = jnp.sum(functools.reduce(jnp.add, [a * b for a, b in zip(w, dp)]), axis=0, keepdims=True) * inv
        ds = [a * (b - delta) for a, b in zip(w, dp)]
        dsp = [jnp.concatenate([a.astype(BF16), b.astype(BF16)], axis=1) for a, b in zip(ds, w)]
        qi = (qt.astype(F32) * inv).astype(BF16)
        di = (dt.astype(F32) * inv).astype(BF16)
        zero = jnp.zeros_like(qi)
        both = jnp.concatenate([jnp.concatenate([qi, zero], axis=1), jnp.concatenate([zero, di], axis=1)], axis=0)
        gr = [lax.dot_general(a, both, NT, preferred_element_type=F32) for a in dsp]
        kt = jnp.concatenate([kvt_ref[h, :, seq_rows(b)] for b in ids], axis=1)
        o = lax.dot_general(kt, jnp.concatenate(dsp, axis=0), NN, preferred_element_type=F32)
        outs.append((gr, o, inv))
    for (h, i, here, there, qt, dt, ids, sd), (gr, o, inv) in zip(st, outs):
        for b, a in zip(ids, gr):
            acc_ref[h, seq_rows(b), :] += a
        g_ref[i // TB, there, :] = (o[:HDIM, :BLK] * (inv * HDIM**-0.5)).astype(BF16)
        at_ref[i // TB, here, :] = (o[HDIM:, BLK:] * inv).astype(BF16)


def make_bias(idx, cnt):
    heads, blocks, slots = idx.shape
    rel = (idx - jnp.arange(blocks)[None, :, None] + REACH) % blocks
    live = jnp.arange(slots) < cnt[:, :, None]
    hit = jnp.any((rel[..., None] == jnp.arange(2 * REACH + 1)) & live[..., None], axis=2)
    return jnp.where(hit, 0.0, -1e30).astype(F32).reshape(-1)


def whole_kernel(scale, bias_ref, q_ref, k_ref, v_ref, dy_ref, w_ref, gr_ref, gw_ref,
                 x_ref, d_ref, wall, at_ref, g_ref, kvt, acc, atr, dyx, part, ring, plane, total, half, other,
                at_s, at_r, fw_s, fw_r, dy_s, dy_r, q_s, q_r, g_s, g_r, z_s, z_r, p_s, p_r, o_s, o_r, loc, *in_sems):
    dp, me = lax.axis_index("dp"), lax.axis_index("seq")
    core, zz, lo = dp % 2, (dp // 2) % 4, dp // 8
    sib = dp + 1 - 2 * core
    rounds, ways, nz, four, srows, tcols = part.shape
    peers = at_ref.shape[0]
    slabs = plane.shape[0]
    feats = at_ref.shape[1] // TB
    tb = TB
    cols = dyx.shape[2]
    my = me * 2 + lo

    def at_z(k):
        return lo * 8 + lax.rem(zz + k + nz, nz) * 2 + core

    def plane_peer(k):
        j = lax.rem(my + k, slabs)
        return j, {"dp": (j % 2) * 8 + zz * 2 + core, "seq": j // 2}

    bar = pltpu.get_barrier_semaphore()

    def hello(where):
        pl.semaphore_signal(bar, inc=1, device_id=where, device_id_type=MESH)

    @pl.loop(1, slabs)
    def _(k):
        hello(plane_peer(k)[1])

    hello({"dp": sib})
    hello({"dp": at_z(1)})
    hello({"dp": at_z(-1)})
    pl.semaphore_wait(bar, slabs + 2)

    def remote(src, dst, ssem, rsem, where):
        return pltpu.make_async_remote_copy(
            src_ref=src, dst_ref=dst, send_sem=ssem, recv_sem=rsem, device_id=where, device_id_type=MESH
        )

    heads = acc.shape[0]

    def key_rows(h, t):
        return pl.ds(pl.multiple_of((h * tb + t) * BLK, BLK), BLK)

    def seq_rows(b):
        return pl.ds(pl.multiple_of(b * BLK, BLK), BLK)

    def turn():
        @pl.loop(0, peers * tb)
        def _(j):
            for h in range(heads):
                kvt[h, :, seq_rows(j)] = x_ref[j // tb, key_rows(h, lax.rem(j, tb)), :].T
                acc[h, seq_rows(j), :] = jnp.zeros((BLK, BLK), F32)

    bring_in(turn, q_ref, k_ref, v_ref, dy_ref, w_ref, x_ref, d_ref, g_ref, at_ref, wall, *in_sems)

    def at_copy(k):
        p = lax.rem(me + k, peers)
        return remote(at_ref.at[p], atr.at[0, me], at_s.at[k], at_r.at[k], {"seq": p})

    mine = pl.ds(pl.multiple_of(core * cols, BLK), cols)
    theirs = pl.ds(pl.multiple_of((1 - core) * cols, BLK), cols)
    dy_copy = remote(dy_ref.at[:, theirs], dyx.at[1], dy_s, dy_r, {"dp": sib})
    dy_copy.start()
    own_dy = pltpu.make_async_copy(dy_ref.at[:, mine], dyx.at[0], loc.at[0])
    own_dy.start()

    def q_copy(k):
        p = lax.rem(me + k, peers)
        r = pl.ds(Q_AT, feats * tb)
        return remote(g_ref.at[p, r], gr_ref.at[me, r], q_s.at[k], q_r.at[k], {"seq": p})

    def g_copy(k):
        p = lax.rem(me + k, peers)
        r = pl.ds(0, Q_AT)
        return remote(g_ref.at[p, r], gr_ref.at[me, r], g_s.at[k], g_r.at[k], {"seq": p})

    def forward(s, k):
        return remote(atr.at[0, s], atr.at[1, s], fw_s.at[k], fw_r.at[k], {"dp": sib})

    def group(r, g):
        return lax.rem(me - 2 * r - 1 - g + 2 * peers, peers)

    def place(r, g):
        return lax.rem(2 * r + 1 + g, peers)

    def arrived(r, both=True):
        for g in range(2 if both else 1):
            at_copy(place(r, g)).wait_recv()
            forward(group(r, g), place(r, g)).start()

    def hop(r, w, step):
        up = 1 - 2 * w
        chunk = lax.rem(zz - up * (1 + step) + 2 * nz, nz)
        return remote(
            part.at[r, w, chunk], ring.at[r, w, step], z_s.at[r, w, step], z_r.at[r, w, step], {"dp": at_z(up)}
        )

    def products(r):
        for g in range(2):
            forward(group(r, g), place(r, g)).wait_recv()
        lhs = jnp.concatenate(
            [
                jnp.concatenate(
                    [atr[q, group(r, g), b * feats : (b + 1) * feats, :] for q in range(2) for b in range(tb)],
                    axis=1,
                )
                for g in range(2)
            ],
            axis=0,
        )
        wide_tile = 2 * BLK
        for w in range(ways):
            for c in range(tcols // wide_tile):
                tc = slice(c * wide_tile, (c + 1) * wide_tile)
                rc = slice(w * tcols + c * wide_tile, w * tcols + (c + 1) * wide_tile)
                rhs = jnp.concatenate([dyx[q, :, rc] for q in range(2)], axis=0)
                prod = lax.dot_general(lhs, rhs, NN, preferred_element_type=F32)
                for a in range(four):
                    for z in range(nz):
                        at = (a * nz + z) * srows
                        part[r, w, z, a, :, tc] = prod[at : at + srows].astype(BF16)
            hop(r, w, 0).start()

    def add(r, step):
        for w in range(ways):
            hop(r, w, step).wait_recv()
            chunk = lax.rem(zz - (1 - 2 * w) * (2 + step) + 2 * nz, nz)
            part[r, w, chunk] = (part[r, w, chunk].astype(F32) + ring[r, w, step].astype(F32)).astype(BF16)
            if step < nz - 2:
                hop(r, w, step + 1).start()

    def slab(r, a):
        where = {"dp": (a % 2) * 8 + zz * 2 + core, "seq": group(r, a // 2)}
        return remote(part.at[r, :, zz, a], plane.at[my], p_s.at[r, a], p_r.at[my], where)

    def other_slab(r, a, f):
        @pl.when((group(r, a // 2) != me) | (lo != a % 2))
        def _():
            f(slab(r, a))

    def spread(r):
        add(r, nz - 2)
        for a in range(four):
            other_slab(r, a, lambda c: c.start())

    def settle(k):
        c = lax.rem(me + k, peers)
        for h in range(heads):
            for t in range(tb):
                g_ref[c, key_rows(h, t), :] = acc[h, seq_rows(c * tb + t), :].astype(BF16)

    dy_copy.wait_recv()
    own_dy.wait()

    @pl.loop(0, rounds)
    def _(pair):
        @pl.loop(0, tb)
        def _(u):
            b0 = (me + 1 + 2 * pair) * tb + 2 * u
            attend(
                [(h, lax.rem(b0 + t, peers * tb)) for t in range(2) for h in range(heads)],
                bias_ref, x_ref, d_ref, kvt, acc, at_ref, g_ref,
            )

            @pl.when((u == 0) & (pair > 1))
            def _():
                add(pair - 2, 0)

            @pl.when((u == 1) & (pair > 0))
            def _():
                arrived(pair - 1)

            @pl.when((u == 1) & (pair > 1))
            def _():
                add(pair - 2, 1)

        at_copy(2 * pair + 1).start()
        q_copy(2 * pair + 1).start()

        @pl.when(pair < rounds - 1)
        def _():
            at_copy(2 * pair + 2).start()
            q_copy(2 * pair + 2).start()

        @pl.when(pair > 0)
        def _():
            products(pair - 1)

        @pl.when(pair > 1)
        def _():
            spread(pair - 2)

        @pl.when(pair == rounds - 2)
        def _():
            for k in (3, 4):
                settle(k)
                g_copy(k).start()

    own_at = pltpu.make_async_copy(at_ref.at[me], atr.at[0, me], loc.at[1])
    own_at.start()
    last = rounds - 1
    late = (1, 2, *range(5, peers))
    settle(1)
    settle(2)
    own_at.wait()
    forward(me, 0).start()
    add(last - 1, 0)
    arrived(last, False)
    for k in late:
        if k > 2:
            settle(k)
        g_copy(k).start()
    settle(0)
    own_g = pltpu.make_async_copy(g_ref.at[me], gr_ref.at[me], loc.at[2])
    own_g.start()
    products(last)
    add(last - 1, 1)
    add(last, 0)
    spread(last - 1)
    add(last, 1)
    spread(last)
    total[...] = part[last, :, zz, 2 + lo].astype(F32)

    @pl.loop(1, slabs)
    def _(k):
        j, where = plane_peer(k)
        remote(plane.at[j], plane.at[j], p_s.at[0, 0], p_r.at[j], where).wait_recv()
        total[...] += plane[j].astype(F32)

    rows = gw_ref.shape[0]
    for c in range(2):
        half[c] = total[:, c * rows : (c + 1) * rows, :] * scale
    swap = remote(half.at[1 - core], other, o_s, o_r, {"dp": sib})
    swap.start()
    swap.wait_recv()
    for t in range(ways):
        gw_ref[:, pl.ds(pl.multiple_of(core * cols + t * tcols, BLK), tcols)] = half[core, t]
        gw_ref[:, pl.ds(pl.multiple_of((1 - core) * cols + t * tcols, BLK), tcols)] = other[t]

    swap.wait_send()
    dy_copy.wait_send()
    own_g.wait()
    forward(me, 0).wait_send()

    @pl.loop(1, peers)
    def _(k):
        at_copy(k).wait_send()
        forward(lax.rem(me - k + peers, peers), k).wait_send()
        q_copy(k).wait()
        g_copy(k).wait()

    @pl.loop(0, rounds)
    def _(r):
        for w in range(ways):
            for step in range(nz - 1):
                hop(r, w, step).wait_send()
        for a in range(four):
            other_slab(r, a, lambda c: c.wait_send())


def whole(bias, q, k, v, dy, w, peers, scale):
    rows, depth = dy.shape
    hd = q.shape[1]
    rounds, ways, nz, slabs = 4, 2, 4, 16
    tcols = depth // 2 // ways
    feats = hd // peers
    x = jax.ShapeDtypeStruct((peers, feats // HDIM * rows + TB * feats, BLK), BF16)
    d = jax.ShapeDtypeStruct((peers, TB * feats, BLK), BF16)
    heads, seq = feats // HDIM, peers * TB * BLK
    out_rows = peers * feats // 128
    dma = pltpu.SemaphoreType.DMA
    return pl.pallas_call(
        functools.partial(whole_kernel, scale),
        out_shape=(jax.ShapeDtypeStruct(x.shape, BF16), jax.ShapeDtypeStruct((out_rows, depth), F32)),
        in_specs=[S, V, V, V, V, V],
        out_specs=(V, V),
        scratch_shapes=[
            pltpu.VMEM(x.shape, BF16),
            pltpu.VMEM(d.shape, BF16),
            pltpu.VMEM((2, 2, nz, *w.shape), BF16),
            pltpu.VMEM(d.shape, BF16),
            pltpu.VMEM(x.shape, BF16),
            pltpu.VMEM((heads, BLK, seq), BF16),
            pltpu.VMEM((heads, seq, BLK), F32),
            pltpu.VMEM((2, *d.shape), BF16),
            pltpu.VMEM((2, rows, depth // 2), BF16),
            pltpu.VMEM((rounds, ways, nz, 4, 2 * out_rows, tcols), BF16),
            pltpu.VMEM((rounds, ways, nz - 1, 4, 2 * out_rows, tcols), BF16),
            pltpu.VMEM((slabs, ways, 2 * out_rows, tcols), BF16),
            pltpu.VMEM((ways, 2 * out_rows, tcols), F32),
            pltpu.VMEM((2, ways, out_rows, tcols), F32),
            pltpu.VMEM((ways, out_rows, tcols), F32),
            dma((peers,)), dma((peers,)), dma((peers,)), dma((peers,)), dma, dma,
            dma((peers,)), dma((peers,)), dma((peers,)), dma((peers,)),
            dma((rounds, ways, nz - 1)), dma((rounds, ways, nz - 1)),
            dma((rounds, 4)), dma((slabs,)), dma, dma, dma((3,)),
            dma((peers,)), dma((peers,)), dma((peers,)), dma((peers,)),
            dma((2, 2, 2)), dma((2, 2, 2)), dma, dma, dma((2, 4)), dma((2, 4)), dma((3,)),
        ],
        compiler_params=pltpu.CompilerParams(
            collective_id=0, has_side_effects=True, vmem_limit_bytes=60 * 2**20
        ),
        cost_estimate=cost(4 * rows * depth * hd, q, k, v, dy, x),
        name="whole",
    )(bias, q, k, v, dy, w)


V = pl.BlockSpec(memory_space=pltpu.VMEM)
S = pl.BlockSpec(memory_space=pltpu.SMEM)


def cost(flops, *arrays):
    return pl.CostEstimate(
        flops=flops, bytes_accessed=sum(a.size * a.dtype.itemsize for a in arrays), transcendentals=0
    )


def wide(rows, cols):
    return pl.BlockSpec((rows, cols), lambda t: (0, t))


def local(query, key_states, value_states, grad_out, w_out, block_index, block_count):
    rows, hd = query.shape[1:]
    n_seq, n_dp = lax.axis_size("seq"), lax.axis_size("dp")
    per = hd // HDIM // n_seq
    tiles = n_seq // 2
    cols = hd // tiles
    x_rows = per * rows + TB * per * HDIM
    packed = jax.ShapeDtypeStruct((n_seq, x_rows, BLK), BF16)
    pairs = pl.BlockSpec((2, x_rows, BLK), lambda t: (t, 0, 0))
    flat = jax.ShapeDtypeStruct((rows, hd), BF16)
    q, k, v, dy = query[0], key_states[0], value_states[0], grad_out[0]

    first = lax.axis_index("seq") * per
    idx = lax.dynamic_slice_in_dim(block_index, first, per, 0)
    cnt = lax.dynamic_slice_in_dim(block_count, first, per, 0)
    scale = float(rows * n_seq * n_dp) ** (-0.5)
    gr, gw = whole(make_bias(idx, cnt), q, k, v, dy, w_out, n_seq, scale)
    dq, dk, dv = pl.pallas_call(
        unpack_kernel, out_shape=(flat,) * 3, grid=(tiles,), in_specs=[pairs],
        out_specs=(wide(rows, cols),) * 3, cost_estimate=cost(0, q, k, v, packed), name="unpack",
    )(gr)
    return dq[None], dk[None], dv[None], gw


def solution(mesh):
    tok = P("dp", "seq", None)
    return jax.shard_map(
        local,
        mesh=mesh,
        in_specs=(tok, tok, tok, tok, P("dp", None), P(), P()),
        out_specs=(tok, tok, tok, P(("seq", "dp"), None)),
        check_vma=False,
    )
```

```python
import functools

import jax
import jax.numpy as jnp
from jax import lax
from jax.experimental import pallas as pl
from jax.experimental.pallas import tpu as pltpu
from jax.sharding import PartitionSpec as P

HDIM = 64
BLK = 128
NT = (((1,), (1,)), ((), ()))
NN = (((1,), (0,)), ((), ()))
TN = (((0,), (0,)), ((), ()))
BF16 = jnp.bfloat16
F32 = jnp.float32
MESH = pl.DeviceIdType.MESH
REACH = 4
TB = 3
Q_AT = 1152


def front_kernel(q_ref, k_ref, v_ref, dy_ref, w_ref, xr_ref, dr_ref, xs, ds, wall,
                 x_s, x_r, d_s, d_r, z_s, z_r, y_s, y_r, f_s, f_r, loc):
    dp, me = lax.axis_index("dp"), lax.axis_index("seq")
    core, zz, lo = dp % 2, (dp // 2) % 4, dp // 8
    sib, mate = dp + 1 - 2 * core, dp + 8 - 16 * lo
    peers, nz = xs.shape[0], wall.shape[2]
    rows = q_ref.shape[0]
    feats = q_ref.shape[1] // peers
    part = wall.shape[3] // 2

    def at_z(k):
        return lo * 8 + lax.rem(zz + k + nz, nz) * 2 + core

    bar = pltpu.get_barrier_semaphore()

    def hello(where):
        pl.semaphore_signal(bar, inc=1, device_id=where, device_id_type=MESH)

    @pl.loop(1, peers)
    def _(k):
        hello({"seq": lax.rem(me + k, peers)})

    for where in (sib, mate, at_z(1), at_z(-1)):
        hello({"dp": where})
    pl.semaphore_wait(bar, peers + 3)

    def remote(src, dst, ssem, rsem, where):
        return pltpu.make_async_remote_copy(
            src_ref=src, dst_ref=dst, send_sem=ssem, recv_sem=rsem, device_id=where, device_id_type=MESH
        )

    def row(l):
        return lo if l == 0 else 1 - lo

    def cell(l, k, c=None):
        return wall.at[core if c is None else c, row(l), lax.rem(zz - k + nz, nz)]

    def source(l):
        return w_ref if l == 0 else cell(l, 0)

    def hop(l, up):
        d = 0 if up == 1 else 1
        return remote(source(l), cell(l, 0), z_s.at[l, d, 0], z_r.at[l, d, 0], {"dp": at_z(up)})

    def hop_in(l, up):
        d = 0 if up == 1 else 1
        return remote(cell(l, up), cell(l, up), z_s.at[l, d, 0], z_r.at[l, d, 0], {"dp": at_z(up)})

    def relay(l, up):
        d = 0 if up == 1 else 1
        h = pl.ds(d * part, part)
        c = cell(l, up).at[h]
        return remote(c, c, z_s.at[l, d, 1], z_r.at[l, d, 1], {"dp": at_z(up)})

    def relay_in(l, up):
        d = 0 if up == 1 else 1
        h = pl.ds(d * part, part)
        c = cell(l, 2).at[h]
        return remote(c, c, z_s.at[l, d, 1], z_r.at[l, d, 1], {"dp": at_z(up)})

    def over(l, k):
        return remote(
            w_ref if (l, k) == (0, 0) else cell(l, k), cell(l, k), f_s.at[l, k], f_r.at[l, k], {"dp": sib}
        )

    def over_in(l, k):
        c = cell(l, k, 1 - core)
        return remote(c, c, f_s.at[l, k], f_r.at[l, k], {"dp": sib})

    hop(0, 1).start()
    hop(0, -1).start()
    to_mate = remote(w_ref, cell(0, 0), y_s, y_r, {"dp": mate})
    to_mate.start()
    over(0, 0).start()
    own_w = pltpu.make_async_copy(w_ref, cell(0, 0), loc.at[0])
    own_w.start()

    k, v = k_ref[...], v_ref[...]
    for p in range(peers):
        for j in range(feats // HDIM):
            cols = slice(p * feats + j * HDIM, p * feats + (j + 1) * HDIM)
            xs[p, j * rows : (j + 1) * rows] = jnp.concatenate([k[:, cols], v[:, cols]], axis=1)
    for p in range(0, peers, 2):
        qt = q_ref[:, p * feats : (p + 2) * feats].T
        for i in range(2):
            for t in range(TB):
                at = Q_AT + t * feats
                xs[p + i, at : at + feats] = qt[i * feats : (i + 1) * feats, t * BLK : (t + 1) * BLK]

    def x_copy(k):
        p = lax.rem(me + k, peers)
        return remote(xs.at[p], xr_ref.at[me], x_s.at[k], x_r.at[k], {"seq": p})

    @pl.loop(1, peers)
    def _(k):
        x_copy(k).start()

    own_x = pltpu.make_async_copy(xs.at[me], xr_ref.at[me], loc.at[1])
    own_x.start()
    own_w.wait()

    def d_copy(n, s):
        return remote(ds.at[s], dr_ref.at[me], d_s.at[n], d_r.at[me], {"seq": s})

    def own_d():
        return pltpu.make_async_copy(ds.at[me], dr_ref.at[me], loc.at[2])

    def peer(l, k):
        return row(l) * nz + lax.rem(zz - k + nz, nz)

    def project(n, l, k):
        over_in(l, k).wait_recv()
        s, z = peer(l, k), lax.rem(zz - k + nz, nz)
        w2 = jnp.concatenate([wall[0, row(l), z], wall[1, row(l), z]], axis=0)
        d = lax.dot_general(w2, dy_ref[...], NT, preferred_element_type=F32).astype(BF16)
        for t in range(TB):
            ds[s, t * feats : (t + 1) * feats] = d[:, t * BLK : (t + 1) * BLK]

        @pl.when(s != me)
        def _():
            d_copy(n, s).start()

        @pl.when(s == me)
        def _():
            own_d().start()

    order = [(0, 0), (1, 0), (0, 1), (0, 3), (1, 1), (1, 3), (0, 2), (1, 2)]

    def spread(l):
        hop_in(l, 1).wait_recv()
        relay(l, 1).start()
        over(l, 1).start()
        hop_in(l, -1).wait_recv()
        relay(l, -1).start()
        over(l, 3).start()

    def finish(l):
        relay_in(l, 1).wait_recv()
        relay_in(l, -1).wait_recv()
        over(l, 2).start()

    project(0, *order[0])
    remote(cell(1, 0), cell(1, 0), y_s, y_r, {"dp": mate}).wait_recv()
    hop(1, 1).start()
    hop(1, -1).start()
    over(1, 0).start()
    spread(0)
    project(1, *order[1])
    project(2, *order[2])
    project(3, *order[3])
    spread(1)
    project(4, *order[4])
    project(5, *order[5])
    finish(0)
    project(6, *order[6])
    finish(1)
    project(7, *order[7])

    for l in range(2):
        for up in (1, -1):
            hop(l, up).wait_send()
            relay(l, up).wait_send()
        for k in range(nz):
            over(l, k).wait_send()
    to_mate.wait_send()
    own_x.wait()

    @pl.loop(1, peers)
    def _(k):
        x_copy(k).wait()

    for n, (l, k) in enumerate(order):
        s = peer(l, k)

        @pl.when(s != me)
        def _():
            d_copy(n, s).wait_send()

        @pl.when(s == me)
        def _():
            own_d().wait()

    @pl.loop(1, peers)
    def _(k):
        p = lax.rem(me + k, peers)
        remote(ds.at[p], dr_ref.at[p], d_s.at[0], d_r.at[p], {"seq": p}).wait_recv()


def unpack_kernel(x_ref, q_ref, k_ref, v_ref):
    rows = q_ref.shape[0]
    feats = q_ref.shape[1] // 2
    ks, vs, qs = [], [], []
    for peer in range(2):
        for j in range(feats // HDIM):
            x = x_ref[peer, j * rows : (j + 1) * rows]
            ks.append(x[:, :HDIM])
            vs.append(x[:, HDIM:])
        qs.append(
            jnp.concatenate(
                [x_ref[peer, Q_AT + t * feats : Q_AT + (t + 1) * feats] for t in range(rows // BLK)], axis=1
            )
        )
    q_ref[...] = jnp.concatenate(qs, axis=0).T
    k_ref[...] = jnp.concatenate(ks, axis=1)
    v_ref[...] = jnp.concatenate(vs, axis=1)


def attend(jobs, bias_ref, x_ref, d_ref, kvt_ref, acc_ref, at_ref, g_ref):
    feats = d_ref.shape[1] // TB
    per = TB * BLK
    blocks = x_ref.shape[0] * TB
    width = 2 * REACH + 1
    def seq_rows(b):
        return pl.ds(pl.multiple_of(b * BLK, BLK), BLK)
    st = []
    for h, i in jobs:
        at = (i % TB) * feats + h * HDIM
        here = pl.ds(pl.multiple_of(at, HDIM), HDIM)
        there = pl.ds(pl.multiple_of(Q_AT + at, HDIM), HDIM)
        qt = x_ref[i // TB, there, :] * BF16(HDIM**-0.5)
        dt = d_ref[i // TB, here, :]
        zero = jnp.zeros_like(qt)
        both = jnp.concatenate([jnp.concatenate([qt, zero], axis=1), jnp.concatenate([zero, dt], axis=1)], axis=0)
        ids = [lax.rem(i + o + blocks - REACH, blocks) for o in range(width)]
        sd = [lax.dot_general(x_ref[b // TB, pl.ds(pl.multiple_of(h * per + (b % TB) * BLK, BLK), BLK), :], both, NN, preferred_element_type=F32) for b in ids]
        st.append((h, i, here, there, qt, dt, ids, sd))
    outs = []
    for h, i, here, there, qt, dt, ids, sd in st:
        s = [sd[o][:, :BLK] + bias_ref[(h * blocks + i) * width + o] if o != REACH else sd[o][:, :BLK] for o in range(width)]
        dp = [a[:, BLK:] for a in sd]
        top = jnp.max(functools.reduce(jnp.maximum, s), axis=0, keepdims=True)
        w = [jnp.exp(a - top) for a in s]
        inv = 1.0 / jnp.sum(functools.reduce(jnp.add, w), axis=0, keepdims=True)
        delta = jnp.sum(functools.reduce(jnp.add, [a * b for a, b in zip(w, dp)]), axis=0, keepdims=True) * inv
        ds = [a * (b - delta) for a, b in zip(w, dp)]
        dsp = [jnp.concatenate([a.astype(BF16), b.astype(BF16)], axis=1) for a, b in zip(ds, w)]
        qi = (qt.astype(F32) * inv).astype(BF16)
        di = (dt.astype(F32) * inv).astype(BF16)
        zero = jnp.zeros_like(qi)
        both = jnp.concatenate([jnp.concatenate([qi, zero], axis=1), jnp.concatenate([zero, di], axis=1)], axis=0)
        gr = [lax.dot_general(a, both, NT, preferred_element_type=F32) for a in dsp]
        kt = jnp.concatenate([kvt_ref[h, :, seq_rows(b)] for b in ids], axis=1)
        o = lax.dot_general(kt, jnp.concatenate(dsp, axis=0), NN, preferred_element_type=F32)
        outs.append((gr, o, inv))
    for (h, i, here, there, qt, dt, ids, sd), (gr, o, inv) in zip(st, outs):
        for b, a in zip(ids, gr):
            acc_ref[h, seq_rows(b), :] += a
        g_ref[i // TB, there, :] = (o[:HDIM, :BLK] * (inv * HDIM**-0.5)).astype(BF16)
        at_ref[i // TB, here, :] = (o[HDIM:, BLK:] * inv).astype(BF16)


def make_bias(idx, cnt):
    heads, blocks, slots = idx.shape
    rel = (idx - jnp.arange(blocks)[None, :, None] + REACH) % blocks
    live = jnp.arange(slots) < cnt[:, :, None]
    hit = jnp.any((rel[..., None] == jnp.arange(2 * REACH + 1)) & live[..., None], axis=2)
    return jnp.where(hit, 0.0, -1e30).astype(F32).reshape(-1)


def rest_kernel(scale, bias_ref, x_ref, d_ref, dy_ref, gr_ref, gw_ref, at_ref, g_ref, kvt, acc, atr, dyx, part, ring, plane, total, half, other,
                at_s, at_r, fw_s, fw_r, dy_s, dy_r, q_s, q_r, g_s, g_r, z_s, z_r, p_s, p_r, o_s, o_r, loc):
    dp, me = lax.axis_index("dp"), lax.axis_index("seq")
    core, zz, lo = dp % 2, (dp // 2) % 4, dp // 8
    sib = dp + 1 - 2 * core
    rounds, ways, nz, four, srows, tcols = part.shape
    peers = at_ref.shape[0]
    slabs = plane.shape[0]
    feats = at_ref.shape[1] // TB
    tb = TB
    cols = dyx.shape[2]
    my = me * 2 + lo

    def at_z(k):
        return lo * 8 + lax.rem(zz + k + nz, nz) * 2 + core

    def plane_peer(k):
        j = lax.rem(my + k, slabs)
        return j, {"dp": (j % 2) * 8 + zz * 2 + core, "seq": j // 2}

    bar = pltpu.get_barrier_semaphore()

    def hello(where):
        pl.semaphore_signal(bar, inc=1, device_id=where, device_id_type=MESH)

    @pl.loop(1, slabs)
    def _(k):
        hello(plane_peer(k)[1])

    hello({"dp": sib})
    hello({"dp": at_z(1)})
    hello({"dp": at_z(-1)})
    pl.semaphore_wait(bar, slabs + 2)

    def remote(src, dst, ssem, rsem, where):
        return pltpu.make_async_remote_copy(
            src_ref=src, dst_ref=dst, send_sem=ssem, recv_sem=rsem, device_id=where, device_id_type=MESH
        )

    def at_copy(k):
        p = lax.rem(me + k, peers)
        return remote(at_ref.at[p], atr.at[0, me], at_s.at[k], at_r.at[k], {"seq": p})

    mine = pl.ds(pl.multiple_of(core * cols, BLK), cols)
    theirs = pl.ds(pl.multiple_of((1 - core) * cols, BLK), cols)
    dy_copy = remote(dy_ref.at[:, theirs], dyx.at[1], dy_s, dy_r, {"dp": sib})
    dy_copy.start()
    own_dy = pltpu.make_async_copy(dy_ref.at[:, mine], dyx.at[0], loc.at[0])
    own_dy.start()

    heads = acc.shape[0]

    def q_copy(k):
        p = lax.rem(me + k, peers)
        r = pl.ds(Q_AT, feats * tb)
        return remote(g_ref.at[p, r], gr_ref.at[me, r], q_s.at[k], q_r.at[k], {"seq": p})

    def g_copy(k):
        p = lax.rem(me + k, peers)
        r = pl.ds(0, Q_AT)
        return remote(g_ref.at[p, r], gr_ref.at[me, r], g_s.at[k], g_r.at[k], {"seq": p})

    def forward(s, k):
        return remote(atr.at[0, s], atr.at[1, s], fw_s.at[k], fw_r.at[k], {"dp": sib})

    def group(r, g):
        return lax.rem(me - 2 * r - 1 - g + 2 * peers, peers)

    def place(r, g):
        return lax.rem(2 * r + 1 + g, peers)

    def arrived(r, both=True):
        for g in range(2 if both else 1):
            at_copy(place(r, g)).wait_recv()
            forward(group(r, g), place(r, g)).start()

    def hop(r, w, step):
        up = 1 - 2 * w
        chunk = lax.rem(zz - up * (1 + step) + 2 * nz, nz)
        return remote(
            part.at[r, w, chunk], ring.at[r, w, step], z_s.at[r, w, step], z_r.at[r, w, step], {"dp": at_z(up)}
        )

    def products(r):
        for g in range(2):
            forward(group(r, g), place(r, g)).wait_recv()
        lhs = jnp.concatenate(
            [
                jnp.concatenate(
                    [atr[q, group(r, g), b * feats : (b + 1) * feats, :] for q in range(2) for b in range(tb)],
                    axis=1,
                )
                for g in range(2)
            ],
            axis=0,
        )
        wide_tile = 2 * BLK
        for w in range(ways):
            for c in range(tcols // wide_tile):
                tc = slice(c * wide_tile, (c + 1) * wide_tile)
                rc = slice(w * tcols + c * wide_tile, w * tcols + (c + 1) * wide_tile)
                rhs = jnp.concatenate([dyx[q, :, rc] for q in range(2)], axis=0)
                prod = lax.dot_general(lhs, rhs, NN, preferred_element_type=F32)
                for a in range(four):
                    for z in range(nz):
                        at = (a * nz + z) * srows
                        part[r, w, z, a, :, tc] = prod[at : at + srows].astype(BF16)
            hop(r, w, 0).start()

    def add(r, step):
        for w in range(ways):
            hop(r, w, step).wait_recv()
            chunk = lax.rem(zz - (1 - 2 * w) * (2 + step) + 2 * nz, nz)
            part[r, w, chunk] = (part[r, w, chunk].astype(F32) + ring[r, w, step].astype(F32)).astype(BF16)
            if step < nz - 2:
                hop(r, w, step + 1).start()

    def slab(r, a):
        where = {"dp": (a % 2) * 8 + zz * 2 + core, "seq": group(r, a // 2)}
        return remote(part.at[r, :, zz, a], plane.at[my], p_s.at[r, a], p_r.at[my], where)

    def other_slab(r, a, f):
        @pl.when((group(r, a // 2) != me) | (lo != a % 2))
        def _():
            f(slab(r, a))

    def spread(r):
        add(r, nz - 2)
        for a in range(four):
            other_slab(r, a, lambda c: c.start())

    def key_rows(h, t):
        return pl.ds(pl.multiple_of((h * tb + t) * BLK, BLK), BLK)

    def seq_rows(b):
        return pl.ds(pl.multiple_of(b * BLK, BLK), BLK)

    @pl.loop(0, peers * tb)
    def _(j):
        for h in range(heads):
            kvt[h, :, seq_rows(j)] = x_ref[j // tb, key_rows(h, lax.rem(j, tb)), :].T
            acc[h, seq_rows(j), :] = jnp.zeros((BLK, BLK), F32)

    def settle(k):
        c = lax.rem(me + k, peers)
        for h in range(heads):
            for t in range(tb):
                g_ref[c, key_rows(h, t), :] = acc[h, seq_rows(c * tb + t), :].astype(BF16)

    dy_copy.wait_recv()
    own_dy.wait()

    @pl.loop(0, peers)
    def _(n):
        b0 = (me + 1 + n) * tb
        attend(
            [(h, lax.rem(b0 + t, peers * tb)) for t in range(tb) for h in range(heads)],
            bias_ref, x_ref, d_ref, kvt, acc, at_ref, g_ref,
        )
        even = n % 2 == 0

        @pl.when(n < peers - 1)
        def _():
            at_copy(n + 1).start()

        @pl.when(even & (n > 3))
        def _():
            add((n - 4) // 2, 1)

        @pl.when((n % 2 == 1) & (n > 2))
        def _():
            add((n - 3) // 2, 0)

        @pl.when(even & (n > 1))
        def _():
            arrived((n - 2) // 2)
            products((n - 2) // 2)

        @pl.when((n % 2 == 1) & (n > 4))
        def _():
            spread((n - 5) // 2)

        @pl.when(n < peers - 1)
        def _():
            q_copy(n + 1).start()

        @pl.when((n > 3) & (n < peers - 1))
        def _():
            settle(n - 1)
            g_copy(n - 1).start()

    own_at = pltpu.make_async_copy(at_ref.at[me], atr.at[0, me], loc.at[1])
    own_at.start()
    last = rounds - 1
    arrived(last, False)
    own_at.wait()
    forward(me, 0).start()
    add(last - 1, 1)
    products(last)
    for k in (1, 2, peers - 2, peers - 1):
        settle(k)
        g_copy(k).start()
    spread(last - 1)
    settle(0)
    own_g = pltpu.make_async_copy(g_ref.at[me], gr_ref.at[me], loc.at[2])
    own_g.start()
    add(last, 0)
    add(last, 1)
    spread(last)
    total[...] = part[last, :, zz, 2 + lo].astype(F32)

    @pl.loop(1, slabs)
    def _(k):
        j, where = plane_peer(k)
        remote(plane.at[j], plane.at[j], p_s.at[0, 0], p_r.at[j], where).wait_recv()
        total[...] += plane[j].astype(F32)

    rows = gw_ref.shape[0]
    for c in range(2):
        half[c] = total[:, c * rows : (c + 1) * rows, :] * scale
    swap = remote(half.at[1 - core], other, o_s, o_r, {"dp": sib})
    swap.start()
    swap.wait_recv()
    for t in range(ways):
        gw_ref[:, pl.ds(pl.multiple_of(core * cols + t * tcols, BLK), tcols)] = half[core, t]
        gw_ref[:, pl.ds(pl.multiple_of((1 - core) * cols + t * tcols, BLK), tcols)] = other[t]

    swap.wait_send()
    dy_copy.wait_send()
    own_g.wait()
    forward(me, 0).wait_send()

    @pl.loop(1, peers)
    def _(k):
        at_copy(k).wait_send()
        forward(lax.rem(me - k + peers, peers), k).wait_send()
        q_copy(k).wait()
        g_copy(k).wait()

    @pl.loop(0, rounds)
    def _(r):
        for w in range(ways):
            for step in range(nz - 1):
                hop(r, w, step).wait_send()
        for a in range(four):
            other_slab(r, a, lambda c: c.wait_send())


def rest(bias, x, d, dy, scale):
    peers = x.shape[0]
    rows, depth = dy.shape
    rounds, ways, nz, slabs = 4, 2, 4, 16
    tcols = depth // 2 // ways
    feats = d.shape[1] // TB
    heads, seq = feats // HDIM, peers * TB * BLK
    out_rows = peers * feats // 128
    dma = pltpu.SemaphoreType.DMA
    return pl.pallas_call(
        functools.partial(rest_kernel, scale),
        out_shape=(jax.ShapeDtypeStruct(x.shape, BF16), jax.ShapeDtypeStruct((out_rows, depth), F32)),
        in_specs=[S, V, V, V],
        out_specs=(V, V),
        scratch_shapes=[
            pltpu.VMEM(d.shape, BF16),
            pltpu.VMEM(x.shape, BF16),
            pltpu.VMEM((heads, BLK, seq), BF16),
            pltpu.VMEM((heads, seq, BLK), F32),
            pltpu.VMEM((2, *d.shape), BF16),
            pltpu.VMEM((2, rows, depth // 2), BF16),
            pltpu.VMEM((rounds, ways, nz, 4, 2 * out_rows, tcols), BF16),
            pltpu.VMEM((rounds, ways, nz - 1, 4, 2 * out_rows, tcols), BF16),
            pltpu.VMEM((slabs, ways, 2 * out_rows, tcols), BF16),
            pltpu.VMEM((ways, 2 * out_rows, tcols), F32),
            pltpu.VMEM((2, ways, out_rows, tcols), F32),
            pltpu.VMEM((ways, out_rows, tcols), F32),
            dma((peers,)), dma((peers,)), dma((peers,)), dma((peers,)), dma, dma,
            dma((peers,)), dma((peers,)), dma((peers,)), dma((peers,)),
            dma((rounds, ways, nz - 1)), dma((rounds, ways, nz - 1)),
            dma((rounds, 4)), dma((slabs,)), dma, dma, dma((3,)),
        ],
        compiler_params=pltpu.CompilerParams(
            collective_id=1, has_side_effects=True, vmem_limit_bytes=60 * 2**20
        ),
        cost_estimate=cost(2 * rows * depth * peers * feats, x, d, x, dy),
        name="rest",
    )(bias, x, d, dy)


V = pl.BlockSpec(memory_space=pltpu.VMEM)
S = pl.BlockSpec(memory_space=pltpu.SMEM)


def cost(flops, *arrays):
    return pl.CostEstimate(
        flops=flops, bytes_accessed=sum(a.size * a.dtype.itemsize for a in arrays), transcendentals=0
    )


def wide(rows, cols):
    return pl.BlockSpec((rows, cols), lambda t: (0, t))


def local(query, key_states, value_states, grad_out, w_out, block_index, block_count):
    rows, hd = query.shape[1:]
    depth = grad_out.shape[2]
    n_seq, n_dp = lax.axis_size("seq"), lax.axis_size("dp")
    per = hd // HDIM // n_seq
    tiles = n_seq // 2
    cols = hd // tiles
    x_rows = per * rows + TB * per * HDIM
    d_rows = TB * per * HDIM
    packed = jax.ShapeDtypeStruct((n_seq, x_rows, BLK), BF16)
    small = jax.ShapeDtypeStruct((n_seq, d_rows, BLK), BF16)
    pairs = pl.BlockSpec((2, x_rows, BLK), lambda t: (t, 0, 0))
    flat = jax.ShapeDtypeStruct((rows, hd), BF16)
    q, k, v, dy = query[0], key_states[0], value_states[0], grad_out[0]

    dma = pltpu.SemaphoreType.DMA
    x, d = pl.pallas_call(
        front_kernel,
        out_shape=(packed, small),
        in_specs=[V] * 5,
        out_specs=(V, V),
        scratch_shapes=[
            pltpu.VMEM(packed.shape, BF16),
            pltpu.VMEM(small.shape, BF16),
            pltpu.VMEM((2, 2, n_dp // 4, *w_out.shape), BF16),
            dma((n_seq,)), dma((n_seq,)), dma((n_seq,)), dma((n_seq,)),
            dma((2, 2, 2)), dma((2, 2, 2)), dma, dma, dma((2, 4)), dma((2, 4)), dma((3,)),
        ],
        compiler_params=pltpu.CompilerParams(
            collective_id=0, has_side_effects=True, vmem_limit_bytes=56 * 2**20
        ),
        cost_estimate=cost(2 * rows * depth * hd, q, k, v, dy, packed),
        name="front",
    )(q, k, v, dy, w_out)
    first = lax.axis_index("seq") * per
    idx = lax.dynamic_slice_in_dim(block_index, first, per, 0)
    cnt = lax.dynamic_slice_in_dim(block_count, first, per, 0)
    scale = float(rows * n_seq * n_dp) ** (-0.5)
    gr, gw = rest(make_bias(idx, cnt), x, d, dy, scale)
    dq, dk, dv = pl.pallas_call(
        unpack_kernel, out_shape=(flat,) * 3, grid=(tiles,), in_specs=[pairs],
        out_specs=(wide(rows, cols),) * 3, cost_estimate=cost(0, q, k, v, packed), name="unpack",
    )(gr)
    return dq[None], dk[None], dv[None], gw


def solution(mesh):
    tok = P("dp", "seq", None)
    return jax.shard_map(
        local,
        mesh=mesh,
        in_specs=(tok, tok, tok, tok, P("dp", None), P(), P()),
        out_specs=(tok, tok, tok, P(("seq", "dp"), None)),
        check_vma=False,
    )
```
